32 devices in a mesh: seq: 8 (over z, y), head: 4 (over x, core).
Axes of the slice: x: 2, y: 2, z: 4, core: 2. Of those that a mesh axis runs over, the one named last changes fastest.
Arguments:
- mamba_inner: bfloat16 [1024, 3072], P('seq', 'head'), may hold values from -6 to 6
- mamba_groups: bfloat16 [1024, 512], P('seq'), may hold values from -6 to 6
- selective_gate: bfloat16 [1024, 3072], P('seq', 'head'), may hold values from -6 to 6
- step_raw: float32 [48, 1024], P('head', 'seq'), may hold values from -3 to 3
- step_bias: float32 [48], P('head'), may hold values from -0.5 to 0.5
- decay_log: float32 [48], P('head'), may hold values from -12 to -2
- conv_inner: float32 [4, 3072], P(None, 'head'), may hold values from -3 to 3
- conv_groups: float32 [4, 512], replicated, may hold values from -3 to 3
- gated_norm_gain: float32 [3072], P('head'), may hold values from 0.1 to 1.9
- query_rows: bfloat16 [1024, 1024], P('seq', 'head'), may hold values from -8 to 8
- key_rows: bfloat16 [1024, 256], P('seq'), may hold values from -8 to 8
- value_rows: bfloat16 [1024, 256], P('seq'), may hold values from -6 to 6
- segment_ids: int32 [1024], P('seq'), may hold values from 0 to 15, never falling along the last dimension, each value on 1 to 682 neighbouring positions
- mamba_proj: bfloat16 [3072, 2048], P('head'), may hold values from -0.109375 to 0.109375
- attn_proj: bfloat16 [1024, 2048], P('head'), may hold values from -0.1875 to 0.1875
Outputs:
- mixed: bfloat16 [1024, 2048], P('seq', 'head')
The draws below stay inside these ranges and needn't reach their ends.
Inputs may be any that keep to these rules, and one draw needn't show every extreme that they name: `segment_ids`: prompt numbers never fall along the tokens; each prompt holds 1 to 682 tokens and one holds exactly 682.
All inputs are finite; a program needn't handle non-finite values.
Results may differ from the reference program's by a relative error of at most 0.015.
Values may be sent and summed in bfloat16 or wider, within the bound.
A program may use at most 128 MiB of HBM per device.

```python
import math
import jax
import jax.numpy as jnp
import numpy as np
from jax import lax

D = 2048
MAMBA_HEADS = 48
HEAD_CHANNELS = 64
STATE_SIZE = 256
KCONV = 4
QH = 8
KVH = 2
HD = 128
BLOCK_TOKENS = 128
SEGS = 16
MAMBA_CHANNELS = 3072
PACKED_TOKENS = 1024
LONGEST = 682
N_SEQ = 8


def draw_decay_log(key, part):
    slow_share = 0.5
    slow = jax.random.uniform(jax.random.fold_in(key, 1), (MAMBA_HEADS,)) < slow_share
    slow_rate = jax.random.uniform(jax.random.fold_in(key, 2), (MAMBA_HEADS,), minval=0.3, maxval=1.5) / LONGEST
    fast_rate = jnp.exp(jax.random.uniform(jax.random.fold_in(key, 3), (MAMBA_HEADS,), minval=math.log(0.01), maxval=math.log(0.08)))
    return jnp.log(jnp.where(slow, slow_rate, fast_rate)).astype(jnp.float32)


def draw_step_raw(key, part):
    piece = max(BLOCK_TOKENS // 2, 1)
    pieces = (PACKED_TOKENS + piece - 1) // piece
    offsets = jax.random.uniform(jax.random.fold_in(key, 21), (MAMBA_HEADS, pieces), minval=-2.5, maxval=2.5)
    spread = jnp.repeat(offsets, piece, axis=1)[:, :PACKED_TOKENS]
    noise = jnp.clip(0.5 * jax.random.normal(jax.random.fold_in(key, 22), (MAMBA_HEADS, PACKED_TOKENS), jnp.float32), -1.5, 1.5)
    return jnp.clip(spread + noise, -3.0, 3.0).astype(jnp.float32)


def extreme_signs(key, salt, shape):
    return jnp.where(jax.random.bernoulli(jax.random.fold_in(key, salt), 0.5, shape), 8.0, -8.0).astype(jnp.float32)


def draw_key_rows(key, part):
    base = jnp.clip(jax.random.normal(jax.random.fold_in(key, 5), (PACKED_TOKENS, KVH * HD), jnp.float32), -6.0, 6.0)
    order = jnp.arange(PACKED_TOKENS)
    columns = jnp.arange(KVH * HD)
    heavy = (order % 257 == 11)[:, None] & (columns < HD)[None, :]
    base = jnp.where(heavy, extreme_signs(key, 31, (PACKED_TOKENS, KVH * HD)), base)
    return base.astype(jnp.bfloat16)


def draw_query_rows(key, part):
    base = jnp.clip(jax.random.normal(jax.random.fold_in(key, 9), (PACKED_TOKENS, QH * HD), jnp.float32), -6.0, 6.0)
    order = jnp.arange(PACKED_TOKENS)
    columns = jnp.arange(QH * HD)
    heavy = (order % 31 == 17)[:, None] & (columns < QH // KVH * HD)[None, :]
    base = jnp.where(heavy, extreme_signs(key, 33, (PACKED_TOKENS, QH * HD)), base)
    return base.astype(jnp.bfloat16)


def levels(stream_key, shape, cuts, smallest, largest):
    level = 1.0
    for axis_at, shards_of in cuts:
        draws = jax.random.uniform(jax.random.fold_in(jax.random.fold_in(stream_key, 6), axis_at), (shards_of,), jnp.float32, smallest / len(cuts), largest / len(cuts))
        level = level * jnp.repeat(jnp.exp(draws), shape[axis_at] // shards_of).reshape((-1,) + (1,) * (len(shape) - 1 - axis_at))
    return level


def length_profile(count, total, bound, skew):
    weights = [(1 << 20) // math.isqrt(grade ** skew) + 1 for grade in range(2, count + 1)]
    spare, holding = total - bound - (count - 1), [1] * (count - 1)
    while spare > 0:
        free = [i for i in range(count - 1) if holding[i] < bound]
        mass, budget = sum([weights[i] for i in free]), spare
        for i in free:
            extra = min(bound - holding[i], max(1, budget * weights[i] // mass), spare)
            holding[i] = holding[i] + extra
            spare = spare - extra
    return np.array([bound] + holding)


def ragged_sizes(own_key, count, total, most, slope):
    if count == 2:
        one = jax.random.randint(own_key, (), max(1, total - most), min(most, total - 1) + 1)
        return jnp.stack([one, total - one])
    sizes = jnp.asarray(length_profile(count, total, most, slope), jnp.int32)
    couples = (count - 1) // 2
    donor, taker = sizes[1:1 + 2 * couples:2], sizes[2:2 + 2 * couples:2]
    slack = jnp.minimum(donor - 1, most - taker)
    moved = jax.random.randint(jax.random.fold_in(own_key, 1), (couples,), 0, 1 << 20) % (slack + 1)
    sizes = sizes.at[1:1 + 2 * couples:2].set(donor - moved).at[2:2 + 2 * couples:2].set(taker + moved)
    return sizes[jax.random.permutation(jax.random.fold_in(own_key, 2), count)]


def gaussian(stream_key, shape, deviation, bound, shards=(), kind=jnp.bfloat16):
    factor_of = levels(stream_key, shape, shards, -0.22, 0.18) if shards else 1.0
    entries = jax.random.normal(stream_key, shape, jnp.float32) * deviation * factor_of
    return jnp.minimum(jnp.maximum(entries, -bound), bound).astype(kind)


def setup_inputs(seed: int = 0) -> dict:
    key_list = jax.random.split(jax.random.key(seed), 16)
    mamba_inner = gaussian(key_list[0], (PACKED_TOKENS, MAMBA_CHANNELS), 1.0, 6.0, ((0, 8), (1, 4)))
    mamba_groups = gaussian(key_list[1], (PACKED_TOKENS, 2 * STATE_SIZE), 1.0, 6.0, ((0, 8),))
    selective_gate = gaussian(key_list[2], (PACKED_TOKENS, MAMBA_CHANNELS), 1.0, 6.0, ((0, 8), (1, 4)))
    step_raw = draw_step_raw(jax.random.fold_in(key_list[15], 71), 0)
    step_bias = jnp.clip(jax.random.uniform(key_list[4], (MAMBA_HEADS,), jnp.float32, -0.5, 0.5) * levels(key_list[4], (MAMBA_HEADS,), ((0, 4),), -0.4, 0.0), -0.5, 0.5)
    decay_log = draw_decay_log(jax.random.fold_in(key_list[15], 71), 0)
    conv_inner = gaussian(key_list[6], (KCONV, MAMBA_CHANNELS), 0.5, 3.0, ((1, 4),), jnp.float32)
    conv_groups = gaussian(key_list[7], (KCONV, 2 * STATE_SIZE), 0.5, 3.0, (), jnp.float32)
    gated_norm_gain = jnp.clip(1.0 + 0.18 * jax.random.normal(key_list[8], (MAMBA_CHANNELS,), jnp.float32), 0.1, 1.9)
    query_rows = draw_query_rows(jax.random.fold_in(key_list[15], 71), 0)
    key_rows = draw_key_rows(jax.random.fold_in(key_list[15], 71), 0)
    value_rows = gaussian(key_list[11], (PACKED_TOKENS, KVH * HD), 1.0, 6.0, ((0, 8),))
    segment_ids = jnp.searchsorted(jnp.cumsum(ragged_sizes(key_list[12], SEGS, PACKED_TOKENS, LONGEST, 2)), jnp.arange(PACKED_TOKENS), side="right").astype(jnp.int32)
    mamba_proj = gaussian(key_list[13], (MAMBA_CHANNELS, D), MAMBA_CHANNELS ** -0.5, 0.109375, ((0, 4),))
    attn_proj = gaussian(key_list[14], (QH * HD, D), (QH * HD) ** -0.5, 0.1875, ((0, 4),))
    return {"mamba_inner": mamba_inner, "mamba_groups": mamba_groups, "selective_gate": selective_gate, "step_raw": step_raw, "step_bias": step_bias, "decay_log": decay_log, "conv_inner": conv_inner, "conv_groups": conv_groups, "gated_norm_gain": gated_norm_gain, "query_rows": query_rows, "key_rows": key_rows, "value_rows": value_rows, "segment_ids": segment_ids, "mamba_proj": mamba_proj, "attn_proj": attn_proj}


def conv_silu(rows, weight, segs, rim_rows, rim_segs):
    item_count = rows.shape[0]
    padded = jnp.concatenate([rim_rows.astype(jnp.float32), rows.astype(jnp.float32)], 0)
    seg_pad = jnp.concatenate([rim_segs, segs], 0)
    total = jnp.zeros(rows.shape, jnp.float32)
    for offset in range(weight.shape[0]):
        window = padded[offset:offset + item_count]
        keep = (seg_pad[offset:offset + item_count] == segs).astype(jnp.float32)
        total = total + weight[offset][None, :] * window * keep[:, None]
    return jax.nn.silu(total).astype(jnp.bfloat16)

def mamba_local(inner, groups, segs, steps, rates, prev_last):
    highest = lax.Precision.HIGHEST
    cumul = jnp.cumsum(-steps * rates[:, None], axis=1)
    read_b = groups[:, :STATE_SIZE]
    read_c = groups[:, STATE_SIZE:]
    intersection = jnp.dot(read_c, read_b.T, preferred_element_type=jnp.float32)
    order = jnp.arange(segs.shape[0], dtype=jnp.int32)
    live = (segs[:, None] == segs[None, :]) & (order[:, None] >= order[None, :])
    decays = jnp.exp(jnp.where(live[None], cumul[:, :, None] - cumul[:, None, :], -jnp.inf))
    mixing = intersection[None] * decays
    scaled = inner.astype(jnp.float32) * steps.T[:, :, None]
    output = jnp.einsum('htj,jhd->thd', mixing, scaled, precision=highest)
    tail = jnp.exp(cumul[:, -1:] - cumul) * (segs == segs[-1]).astype(jnp.float32)[None, :]
    local_state = jnp.einsum('ht,thd,tn->hdn', tail, scaled, read_b.astype(jnp.float32), precision=highest)
    through = jnp.exp(cumul[:, -1]) * (segs[-1] == prev_last).astype(jnp.float32)
    return (output, through, local_state, cumul)

def mamba_incoming(output, incoming, groups, segs, cumul, prev_last):
    read_c = groups[:, STATE_SIZE:].astype(jnp.float32)
    joined = (segs == prev_last).astype(jnp.float32)
    from_carry = jnp.einsum('hdn,tn->thd', incoming, read_c, precision=lax.Precision.HIGHEST)
    return output + jnp.exp(cumul).T[:, :, None] * joined[:, None, None] * from_carry

def reference(mamba_inner, mamba_groups, selective_gate, step_raw, step_bias, decay_log, conv_inner, conv_groups, gated_norm_gain, query_rows, key_rows, value_rows, segment_ids, mamba_proj, attn_proj):
    segs = segment_ids
    zero_segs = jnp.zeros((KCONV - 1,), jnp.int32)
    inner_filtered = conv_silu(mamba_inner, conv_inner, segs, jnp.zeros((KCONV - 1, MAMBA_CHANNELS), jnp.float32), zero_segs)
    groups_conv = conv_silu(mamba_groups, conv_groups, segs, jnp.zeros((KCONV - 1, 2 * STATE_SIZE), jnp.float32), zero_segs)
    steps = jax.nn.softplus(step_raw + step_bias[:, None])
    rates = jnp.exp(decay_log)
    inner_block_rows = inner_filtered.reshape(N_SEQ, BLOCK_TOKENS, MAMBA_HEADS, HEAD_CHANNELS)
    group_blocks = groups_conv.reshape(N_SEQ, BLOCK_TOKENS, 2 * STATE_SIZE)
    seg_blocks = segs.reshape(N_SEQ, BLOCK_TOKENS)
    step_blocks = steps.reshape(MAMBA_HEADS, N_SEQ, BLOCK_TOKENS).transpose(1, 0, 2)

    def advance(carry, block):
        state, prev_last = carry
        inner, groups, block_segs, block_steps = block
        output, through, local_state, cumul = mamba_local(inner, groups, block_segs, block_steps, rates, prev_last)
        output = mamba_incoming(output, state, groups, block_segs, cumul, prev_last)
        return ((through[:, None, None] * state + local_state, block_segs[-1]), output)
    initial_carry = (jnp.zeros((MAMBA_HEADS, HEAD_CHANNELS, STATE_SIZE), jnp.float32), jnp.zeros((), jnp.int32))
    final_carry, mixer_outputs = lax.scan(advance, initial_carry, (inner_block_rows, group_blocks, seg_blocks, step_blocks))
    selective_output = mixer_outputs.reshape(PACKED_TOKENS, MAMBA_HEADS, HEAD_CHANNELS)
    gated_values = selective_output * jax.nn.silu(selective_gate.astype(jnp.float32)).reshape(PACKED_TOKENS, MAMBA_HEADS, HEAD_CHANNELS)
    mean_square = lax.optimization_barrier(jnp.mean(gated_values * gated_values, axis=-1, keepdims=True))
    normalized_rows = (gated_values * lax.rsqrt(mean_square + 1e-05) * gated_norm_gain.reshape(MAMBA_HEADS, HEAD_CHANNELS)).astype(jnp.bfloat16).reshape(PACKED_TOKENS, MAMBA_CHANNELS)
    scale = 1.0 / math.sqrt(HD)
    query_blocks = query_rows.reshape(N_SEQ, BLOCK_TOKENS, KVH, QH // KVH, HD)
    keys_all = key_rows.reshape(PACKED_TOKENS, KVH, HD).astype(jnp.float32)
    values_all = value_rows.reshape(PACKED_TOKENS, KVH, HD).astype(jnp.float32)
    positions = jnp.arange(PACKED_TOKENS, dtype=jnp.int32)

    def attend(block):
        queries, index = block
        first = (index * BLOCK_TOKENS).astype(jnp.int32)
        query_pos = first + jnp.arange(BLOCK_TOKENS, dtype=jnp.int32)
        query_seg = lax.dynamic_slice_in_dim(segs, first, BLOCK_TOKENS)
        scores = jnp.einsum('tgrd,kgd->grtk', queries.astype(jnp.float32), keys_all) * scale
        allowed = (segs[None, :] == query_seg[:, None]) & (positions[None, :] <= query_pos[:, None])
        scores = jnp.where(allowed[None, None], scores, -jnp.inf)
        top = lax.optimization_barrier(jnp.max(scores, axis=-1, keepdims=True))
        weights = jnp.exp(scores - top)
        total = lax.optimization_barrier(jnp.sum(weights, axis=-1))
        rounded = lax.optimization_barrier(weights.astype(jnp.bfloat16))
        summed = jnp.einsum('grtk,kgd->tgrd', rounded.astype(jnp.float32), values_all)
        return (summed / total.transpose(2, 0, 1)[..., None]).astype(jnp.bfloat16)
    attended = lax.map(attend, (query_blocks, jnp.arange(N_SEQ, dtype=jnp.int32))).reshape(PACKED_TOKENS, QH * HD)
    terms = jnp.dot(normalized_rows, mamba_proj, preferred_element_type=jnp.float32) + jnp.dot(attended, attn_proj, preferred_element_type=jnp.float32)
    return terms.astype(jnp.bfloat16)
```

```python
import functools
import math

import jax
import jax.numpy as jnp
from jax import lax
from jax.experimental import pallas as pl
from jax.experimental.pallas import tpu as pltpu
from jax.sharding import PartitionSpec as P

HEAD_CHANNELS = 64
STATE_SIZE = 256
QH = 8
KVH = 2
HD = 128
LANES = 128
RIM = 16
F32 = jnp.float32
BF16 = jnp.bfloat16
MESH = pl.DeviceIdType.MESH
HIGHEST = lax.Precision.HIGHEST


def dot(a, b, contract, precision=None):
    return lax.dot_general(
        a, b, ((contract[:1], contract[1:]), ((), ())), precision=precision, preferred_element_type=F32
    )


def iota(shape, axis):
    return lax.broadcasted_iota(jnp.int32, shape, axis)


def column(row):
    n = row.shape[1]
    eye = iota((n, n), 0) == iota((n, n), 1)
    return jnp.sum(jnp.where(eye, jnp.broadcast_to(row, (n, n)), 0.0), axis=1, keepdims=True)


def kernel(
    n_seq,
    n_head,
    inner_ref,
    groups_ref,
    gate_ref,
    step_ref,
    bias_ref,
    decay_ref,
    taps_inner_ref,
    taps_groups_ref,
    gain_ref,
    query_ref,
    key_ref,
    value_ref,
    segs_ref,
    mamba_proj_hbm,
    attn_proj_hbm,
    out_ref,
    mproj,
    aproj,
    pad_inner,
    pad_groups,
    rim_inner,
    rim_groups,
    meta,
    kv,
    conv_x,
    conv_bc,
    cumx,
    y_ref,
    state,
    s_send,
    s_recv,
    e_send,
    e_recv,
    f_send,
    f_recv,
    entering,
    both,
    rs_send,
    rs_recv,
    weight_sem,
    rim_sem,
    meta_ss,
    meta_rs,
    kv_ss,
    kv_rs,
    s_ss,
    s_rs,
    e_ss,
    e_rs,
    f_ss,
    f_rs,
    rs_ss,
    rs_rs,
):
    tokens, channels = inner_ref.shape
    heads = step_ref.shape[0]
    half = channels // 2
    chunks = half // LANES
    pairs = channels // LANES
    me = lax.axis_index("seq")
    mine = lax.axis_index("head")
    pair, side = me // 2, me % 2
    last_pair = n_seq // 2 - 1
    heads_here = query_ref.shape[1] // HD

    def at_seq(s):
        return (s, mine)

    def at_head(h):
        return (me, h)

    weights = [
        pltpu.make_async_copy(mamba_proj_hbm, mproj, weight_sem.at[0]),
        pltpu.make_async_copy(attn_proj_hbm, aproj, weight_sem.at[1]),
    ]
    for w in weights:
        w.start()

    barrier = pltpu.get_barrier_semaphore()
    for d in range(1, n_seq):
        pl.semaphore_signal(barrier, inc=1, device_id=at_seq((me + d) % n_seq), device_id_type=MESH)
    for d in range(1, n_head):
        pl.semaphore_signal(barrier, inc=1, device_id=at_head((mine + d) % n_head), device_id_type=MESH)

    kv_head = mine * heads_here // (QH // KVH)
    kv_cols = pl.ds(pl.multiple_of(kv_head * HD, HD), HD)
    kv[me, :, 0:HD] = key_ref[:, kv_cols]
    kv[me, :, HD : 2 * HD] = value_ref[:, kv_cols]

    raw = step_ref[...] + column(bias_ref[...])
    steps = jnp.maximum(raw, 0.0) + jnp.log1p(jnp.exp(-jnp.abs(raw)))
    rates = jnp.exp(column(decay_ref[...]))
    row_t, col_t = iota((tokens, tokens), 0), iota((tokens, tokens), 1)
    upto = (row_t <= col_t).astype(F32)
    cumul = dot(-steps * rates, upto, (1, 0), HIGHEST)
    spread = (iota((heads, channels), 1) // HEAD_CHANNELS == iota((heads, channels), 0)).astype(F32)
    cumx[...] = dot(cumul, spread, (0, 0), HIGHEST)
    stepx = dot(steps, spread, (0, 0), HIGHEST)
    total_row = cumx[tokens - 1 : tokens, :]
    segs_row = segs_ref[...].astype(F32)
    segs_col = column(segs_row)
    last_seg = segs_row[:, tokens - 1 : tokens]
    meta[me, 0:1, :] = total_row
    meta[me, 1:2, 0:tokens] = segs_row
    meta[me, 2:3, :] = jnp.broadcast_to(last_seg, (1, channels))
    pl.semaphore_wait(barrier, n_seq + n_head - 2)

    def rim_copies(target):
        tail = pl.ds(tokens - RIM, RIM)
        return [
            pltpu.make_async_remote_copy(
                src.at[tail, :], dst, rim_sem.at[0, i], rim_sem.at[1, i], device_id=at_seq(target), device_id_type=MESH
            )
            for i, (src, dst) in enumerate(((inner_ref, rim_inner), (groups_ref, rim_groups)))
        ]

    def meta_copy(slot, other):
        return pltpu.make_async_remote_copy(
            meta.at[slot], meta.at[slot], meta_ss.at[other], meta_rs.at[slot], device_id=at_seq(other), device_id_type=MESH
        )

    def kv_copy(slot, other):
        return pltpu.make_async_remote_copy(
            kv.at[slot], kv.at[slot], kv_ss.at[other], kv_rs.at[slot], device_id=at_seq(other), device_id_type=MESH
        )

    following = lax.min(me + 1, n_seq - 1)
    previous = lax.max(me - 1, 0)

    @pl.when(me < n_seq - 1)
    def _():
        for c in rim_copies(following):
            c.start()

    def send_meta(d, _):
        meta_copy(me, (me + d) % n_seq).start()
        return 0

    lax.fori_loop(1, n_seq, send_meta, 0)

    def send_kv(k, _):
        kv_copy(me, k).start()
        return 0

    lax.fori_loop(me + 1, n_seq, send_kv, 0)

    pad_inner[RIM:, :] = inner_ref[...].astype(F32)
    pad_groups[RIM:, :] = groups_ref[...].astype(F32)

    def wait_meta(d, _):
        k = (me + d) % n_seq
        meta_copy(k, k).wait_recv()
        return 0

    lax.fori_loop(1, n_seq, wait_meta, 0)

    @pl.when(me > 0)
    def _():
        for c in rim_copies(previous):
            c.wait_recv()

    @pl.when(me == 0)
    def _():
        rim_inner[...] = jnp.zeros_like(rim_inner)
        rim_groups[...] = jnp.zeros_like(rim_groups)

    pad_inner[0:RIM, :] = rim_inner[...].astype(F32)
    pad_groups[0:RIM, :] = rim_groups[...].astype(F32)

    taps = taps_inner_ref.shape[0]
    prev_last = meta[previous, 2:3, 0:1]
    prev_segs = meta[previous, 1:2, 0:tokens]
    token_col = iota((tokens, 1), 0)
    keeps = []
    for k in range(taps - 1):
        back = taps - 1 - k
        own = jnp.sum(
            jnp.where(row_t - back == col_t, jnp.broadcast_to(segs_row, (tokens, tokens)), 0.0), 1, keepdims=True
        )
        before = jnp.sum(
            jnp.where(row_t - back + tokens == col_t, jnp.broadcast_to(prev_segs, (tokens, tokens)), 0.0),
            1,
            keepdims=True,
        )
        keeps.append(jnp.where(token_col >= back, own, before) == segs_col)

    def conv(pad, weight_ref, out):
        for c in range(0, out.shape[1], LANES):
            cols = slice(c, c + LANES)
            acc = jnp.zeros((tokens, LANES), F32)
            for k in range(taps):
                first = RIM - (taps - 1) + k
                term = weight_ref[k : k + 1, cols] * pad[first : first + tokens, cols]
                acc = acc + (jnp.where(keeps[k], term, 0.0) if k < taps - 1 else term)
            out[:, cols] = jax.nn.silu(acc).astype(BF16)

    conv(pad_groups, taps_groups_ref, conv_bc)
    conv(pad_inner, taps_inner_ref, conv_x)

    read_b = conv_bc[:, :STATE_SIZE]
    read_c = conv_bc[:, STATE_SIZE:]
    in_last = segs_col == last_seg
    tail = jnp.where(in_last, jnp.exp(total_row - cumx[...]), 0.0)
    weighted = (tail * stepx * conv_x[...].astype(F32)).astype(BF16)
    state[...] = dot(read_b, weighted, (0, 0))

    partner = me + 1 - 2 * side
    upper = lax.min(me + 2, n_seq - 1)
    lower = lax.max(me - 2, 0)

    def part(which, c):
        return pl.ds(pl.multiple_of(which * half + c * LANES, LANES), LANES)

    def hop(src, dst, ss, rs, c, target):
        return pltpu.make_async_remote_copy(
            src.at[c], dst.at[c], ss.at[c], rs.at[c], device_id=at_seq(target), device_id_type=MESH
        )

    for c in range(chunks):
        s_send[c] = state[:, part(1 - side, c)].astype(BF16)
        hop(s_send, s_recv, s_ss, s_rs, c, partner).start()

    crossing = dot(read_c, read_b, (1, 1))
    live = (jnp.broadcast_to(segs_row, (tokens, tokens)) == segs_col) & (row_t >= col_t)
    eye = (iota((heads, heads), 0) == iota((heads, heads), 1)).astype(F32)
    cum_cols = dot(cumul, eye, (0, 0), HIGHEST)
    left = iota((tokens, LANES), 1) < HEAD_CHANNELS
    for p in range(pairs):
        got = []
        for h in (2 * p, 2 * p + 1):
            decays = jnp.exp(jnp.where(live, cum_cols[:, h : h + 1] - cumul[h : h + 1, :], -jnp.inf))
            mixing = (crossing * decays * steps[h : h + 1, :]).astype(BF16)
            got.append(dot(mixing, conv_x[:, p * LANES : (p + 1) * LANES], (1, 0)))
        y_ref[:, p * LANES : (p + 1) * LANES] = jnp.where(left, got[0], got[1])

    scale = 1.0 / math.sqrt(HD)
    queries = jnp.concatenate([query_ref[:, h * HD : (h + 1) * HD] for h in range(heads_here)], axis=0)
    rows = heads_here * tokens
    segs_rows = jnp.concatenate([segs_col] * heads_here, axis=0)
    token_rows = jnp.concatenate([token_col] * heads_here, axis=0)

    def attend(d, carry):
        top, total, summed = carry
        k = me - d

        @pl.when(d > 0)
        def _():
            kv_copy(k, k).wait_recv()

        scores = dot(queries, kv[k, :, 0:HD], (1, 1)) * scale
        allowed = (meta[k, 1:2, 0:tokens] == segs_rows) & (
            iota((rows, tokens), 1) + (k - me) * tokens <= token_rows
        )
        scores = jnp.where(allowed, scores, -jnp.inf)
        new_top = jnp.maximum(top, jnp.max(scores, axis=1, keepdims=True))
        rescale = jnp.exp(top - new_top)
        w = jnp.exp(scores - new_top)
        total = total * rescale + jnp.sum(w, axis=1, keepdims=True)
        summed = summed * rescale + dot(w.astype(BF16), kv[k, :, HD : 2 * HD], (1, 0))
        return new_top, total, summed

    top, total, summed = lax.fori_loop(
        0,
        me + 1,
        attend,
        (jnp.full((rows, 1), -1e30, F32), jnp.zeros((rows, 1), F32), jnp.zeros((rows, HD), F32)),
    )
    attended = (summed / total).astype(BF16)
    for h in range(heads_here):
        both[:, channels + h * HD : channels + (h + 1) * HD] = attended[h * tokens : (h + 1) * tokens]

    @pl.when(pair == 0)
    def _():
        e_recv[...] = jnp.zeros_like(e_recv)

    first, second = pair * 2, pair * 2 + 1
    seg_before = meta[lax.max(first - 1, 0), 2:3, 0:LANES]
    seg_first = meta[first, 2:3, 0:LANES]
    seg_second = meta[second, 2:3, 0:LANES]
    on_left = side == 0
    for c in range(chunks):
        cols = part(side, c)
        through_first = jnp.where(seg_first == seg_before, jnp.exp(meta[first, 0:1, cols]), 0.0)
        through_second = jnp.where(seg_second == seg_first, jnp.exp(meta[second, 0:1, cols]), 0.0)
        hop(s_send, s_recv, s_ss, s_rs, c, partner).wait_recv()
        own, others = state[:, cols], s_recv[c].astype(F32)

        @pl.when(pair > 0)
        def _():
            hop(e_send, e_recv, e_ss, e_rs, c, lower).wait_recv()

        enter_first = e_recv[c].astype(F32)
        enter_second = through_first * enter_first + jnp.where(on_left, own, others)

        @pl.when(pair < last_pair)
        def _():
            e_send[c] = (through_second * enter_second + jnp.where(on_left, others, own)).astype(BF16)
            hop(e_send, e_recv, e_ss, e_rs, c, upper).start()

        f_send[c] = jnp.where(on_left, enter_second, enter_first).astype(BF16)
        hop(f_send, f_recv, f_ss, f_rs, c, partner).start()
        entering[:, cols] = jnp.where(on_left, enter_first, enter_second).astype(BF16)

    for c in range(chunks):
        hop(f_send, f_recv, f_ss, f_rs, c, partner).wait_recv()
        entering[:, part(1 - side, c)] = f_recv[c]

    joined = segs_col == prev_last
    same_head = (iota((LANES, LANES), 0) // HEAD_CHANNELS == iota((LANES, LANES), 1) // HEAD_CHANNELS).astype(F32)
    for p in range(pairs):
        cols = slice(p * LANES, (p + 1) * LANES)
        carried = dot(read_c, entering[:, cols], (1, 0))
        y = y_ref[:, cols] + jnp.where(joined, jnp.exp(cumx[:, cols]), 0.0) * carried
        gated = y * jax.nn.silu(gate_ref[:, cols].astype(F32))
        mean_square = dot(gated * gated, same_head, (1, 0), HIGHEST) * (1.0 / HEAD_CHANNELS)
        both[:, cols] = (gated * lax.rsqrt(mean_square + 1e-05) * gain_ref[:, cols]).astype(BF16)

    for w in weights:
        w.wait()
    width = out_ref.shape[1]

    def product(j):
        cols = pl.ds(pl.multiple_of(j * width, LANES), width)
        return dot(both[:, :channels], mproj[:, cols], (1, 0)) + dot(both[:, channels:], aproj[:, cols], (1, 0))

    def rs_copy(d):
        return pltpu.make_async_remote_copy(
            rs_send.at[d - 1],
            rs_recv.at[d - 1],
            rs_ss.at[d - 1],
            rs_rs.at[d - 1],
            device_id=at_head((mine + d) % n_head),
            device_id_type=MESH,
        )

    turns = sorted(range(1, n_head), key=lambda d: abs(d - n_head // 2))
    for d in turns:
        rs_send[d - 1] = product((mine + d) % n_head).astype(BF16)
        rs_copy(d).start()
    result = product(mine)
    for d in turns:
        rs_copy(d).wait_recv()
        result = result + rs_recv[d - 1].astype(F32)
    out_ref[...] = result.astype(BF16)

    for d in turns:
        rs_copy(d).wait_send()

    @pl.when(me < n_seq - 1)
    def _():
        for c in rim_copies(following):
            c.wait_send()

    def sent_meta(d, _):
        meta_copy(me, (me + d) % n_seq).wait_send()
        return 0

    lax.fori_loop(1, n_seq, sent_meta, 0)

    def sent_kv(k, _):
        kv_copy(me, k).wait_send()
        return 0

    lax.fori_loop(me + 1, n_seq, sent_kv, 0)
    for c in range(chunks):
        hop(s_send, s_recv, s_ss, s_rs, c, partner).wait_send()
        hop(f_send, f_recv, f_ss, f_rs, c, partner).wait_send()

        @pl.when(pair < last_pair)
        def _():
            hop(e_send, e_recv, e_ss, e_rs, c, upper).wait_send()


def shards(n_seq, n_head, *arrays):
    (inner, groups, gate, step, bias, decay, taps_i, taps_g, gain, query, key, value, segs, mproj, aproj) = arrays
    tokens, channels = inner.shape
    out_width = mproj.shape[1] // n_head
    chunks = channels // 2 // LANES
    hops = (chunks, STATE_SIZE, LANES)
    vmem = pl.BlockSpec(memory_space=pltpu.VMEM)
    hbm = pl.BlockSpec(memory_space=pl.ANY)
    dma = pltpu.SemaphoreType.DMA
    scratch = [
        pltpu.VMEM(mproj.shape, BF16),
        pltpu.VMEM(aproj.shape, BF16),
        pltpu.VMEM((tokens + RIM, channels), F32),
        pltpu.VMEM((tokens + RIM, groups.shape[1]), F32),
        pltpu.VMEM((RIM, channels), BF16),
        pltpu.VMEM((RIM, groups.shape[1]), BF16),
        pltpu.VMEM((n_seq, 8, channels), F32),
        pltpu.VMEM((n_seq, tokens, 2 * HD), BF16),
        pltpu.VMEM((tokens, channels), BF16),
        pltpu.VMEM((tokens, groups.shape[1]), BF16),
        pltpu.VMEM((tokens, channels), F32),
        pltpu.VMEM((tokens, channels), F32),
        pltpu.VMEM((STATE_SIZE, channels), F32),
        *[pltpu.VMEM(hops, BF16) for _ in range(6)],
        pltpu.VMEM((STATE_SIZE, channels), BF16),
        pltpu.VMEM((tokens, channels + query.shape[1]), BF16),
        pltpu.VMEM((n_head - 1, tokens, out_width), BF16),
        pltpu.VMEM((n_head - 1, tokens, out_width), BF16),
        dma((2,)),
        dma((2, 2)),
        dma((n_seq,)),
        dma((n_seq,)),
        dma((n_seq,)),
        dma((n_seq,)),
        *[dma((chunks,)) for _ in range(6)],
        dma((n_head - 1,)),
        dma((n_head - 1,)),
    ]
    return pl.pallas_call(
        functools.partial(kernel, n_seq, n_head),
        out_shape=jax.ShapeDtypeStruct((tokens, out_width), BF16),
        in_specs=[vmem] * 13 + [hbm] * 2,
        out_specs=vmem,
        scratch_shapes=scratch,
        compiler_params=pltpu.CompilerParams(
            collective_id=0, has_side_effects=True, vmem_limit_bytes=48 * 2**20
        ),
        name="mixer",
    )(
        inner,
        groups,
        gate,
        step,
        bias.reshape(1, -1),
        decay.reshape(1, -1),
        taps_i,
        taps_g,
        gain.reshape(1, -1),
        query,
        key,
        value,
        segs.reshape(1, -1),
        mproj,
        aproj,
    )


def solution(mesh):
    placed = (
        P("seq", "head"),
        P("seq", None),
        P("seq", "head"),
        P("head", "seq"),
        P("head"),
        P("head"),
        P(None, "head"),
        P(),
        P("head"),
        P("seq", "head"),
        P("seq", None),
        P("seq", None),
        P("seq"),
        P("head", None),
        P("head", None),
    )
    return jax.shard_map(
        functools.partial(shards, mesh.shape["seq"], mesh.shape["head"]),
        mesh=mesh,
        in_specs=placed,
        out_specs=P("seq", "head"),
        check_vma=False,
    )
```

```python
import functools
import math

import jax
import jax.numpy as jnp
from jax import lax
from jax.experimental import pallas as pl
from jax.experimental.pallas import tpu as pltpu
from jax.sharding import PartitionSpec as P

HEAD_CHANNELS = 64
STATE_SIZE = 256
QH = 8
KVH = 2
HD = 128
LANES = 128
RIM = 16
F32 = jnp.float32
BF16 = jnp.bfloat16
MESH = pl.DeviceIdType.MESH
HIGHEST = lax.Precision.HIGHEST


def dot(a, b, contract, precision=None):
    return lax.dot_general(
        a, b, ((contract[:1], contract[1:]), ((), ())), precision=precision, preferred_element_type=F32
    )


def iota(shape, axis):
    return lax.broadcasted_iota(jnp.int32, shape, axis)


def column(row):
    n = row.shape[1]
    eye = iota((n, n), 0) == iota((n, n), 1)
    return jnp.sum(jnp.where(eye, jnp.broadcast_to(row, (n, n)), 0.0), axis=1, keepdims=True)


def kernel(
    n_seq,
    n_head,
    inner_hbm,
    groups_hbm,
    gate_hbm,
    step_hbm,
    bias_hbm,
    decay_hbm,
    taps_inner_hbm,
    taps_groups_hbm,
    gain_hbm,
    query_hbm,
    key_hbm,
    value_hbm,
    segs_hbm,
    mamba_proj_hbm,
    attn_proj_hbm,
    out_ref,
    inner_ref,
    groups_ref,
    gate_ref,
    step_ref,
    bias_ref,
    decay_ref,
    taps_inner_ref,
    taps_groups_ref,
    gain_ref,
    query_ref,
    key_ref,
    value_ref,
    segs_ref,
    mproj,
    aproj,
    pad_inner,
    pad_groups,
    rim_inner,
    rim_groups,
    meta,
    kv,
    conv_x,
    conv_bc,
    cumx,
    y_ref,
    state,
    s_send,
    s_recv,
    e_send,
    e_recv,
    f_send,
    f_recv,
    partner_c,
    carried_ref,
    through,
    both,
    rs_send,
    rs_recv,
    load_sem,
    weight_sem,
    rim_sem,
    meta_ss,
    meta_rs,
    kv_ss,
    kv_rs,
    share_ss,
    share_rs,
    c_ss,
    c_rs,
    s_ss,
    s_rs,
    e_ss,
    e_rs,
    f_ss,
    f_rs,
    rs_ss,
    rs_rs,
):
    tokens, channels = inner_ref.shape
    heads = step_ref.shape[0]
    half = channels // 2
    chunks = half // LANES
    pairs = channels // LANES
    me = lax.axis_index("seq")
    mine = lax.axis_index("head")
    pair, side = me // 2, me % 2
    last_pair = n_seq // 2 - 1
    heads_here = query_ref.shape[1] // HD
    core = mine % 2
    sibling = mine + 1 - 2 * core
    opposite = (mine + 2) % n_head
    opposite_sibling = (sibling + 2) % n_head

    def at_seq(s):
        return (s, mine)

    def at_head(h):
        return (me, h)

    weights = [
        pltpu.make_async_copy(mamba_proj_hbm, mproj, weight_sem.at[0]),
        pltpu.make_async_copy(attn_proj_hbm, aproj, weight_sem.at[1]),
    ]
    loads = [
        pltpu.make_async_copy(src, dst, load_sem.at[i])
        for i, (src, dst) in enumerate(
            (
                (step_hbm, step_ref),
                (bias_hbm, bias_ref),
                (decay_hbm, decay_ref),
                (segs_hbm, segs_ref),
                (key_hbm, key_ref),
                (value_hbm, value_ref),
                (inner_hbm, inner_ref),
                (groups_hbm, groups_ref),
                (taps_inner_hbm, taps_inner_ref),
                (taps_groups_hbm, taps_groups_ref),
                (query_hbm, query_ref),
                (gate_hbm, gate_ref),
                (gain_hbm, gain_ref),
            )
        )
    ]
    for w in loads + weights:
        w.start()

    barrier = pltpu.get_barrier_semaphore()
    for d in range(1, n_seq):
        pl.semaphore_signal(barrier, inc=1, device_id=at_seq((me + d) % n_seq), device_id_type=MESH)
    for d in range(1, n_head):
        pl.semaphore_signal(barrier, inc=1, device_id=at_head((mine + d) % n_head), device_id_type=MESH)

    for w in loads[:6]:
        w.wait()
    kv_head = mine * heads_here // (QH // KVH)
    kv_cols = pl.ds(pl.multiple_of(kv_head * HD, HD), HD)
    kv[me, 0] = key_ref[:, kv_cols]
    kv[me, 1] = value_ref[:, kv_cols]

    raw = step_ref[...] + column(bias_ref[...].reshape(1, heads))
    steps = jnp.maximum(raw, 0.0) + jnp.log1p(jnp.exp(-jnp.abs(raw)))
    rates = jnp.exp(column(decay_ref[...].reshape(1, heads)))
    row_t, col_t = iota((tokens, tokens), 0), iota((tokens, tokens), 1)
    upto = (row_t <= col_t).astype(F32)
    cumul = dot(-steps * rates, upto, (1, 0), HIGHEST)
    spread = (iota((heads, channels), 1) // HEAD_CHANNELS == iota((heads, channels), 0)).astype(F32)
    cumx[...] = dot(cumul, spread, (0, 0), HIGHEST)
    stepx = dot(steps, spread, (0, 0), HIGHEST)
    total_row = cumx[tokens - 1 : tokens, :]
    segs_row = segs_ref[...].reshape(1, tokens).astype(F32)
    segs_col = column(segs_row)
    last_seg = segs_row[:, tokens - 1 : tokens]
    eye = (iota((heads, heads), 0) == iota((heads, heads), 1)).astype(F32)
    cum_cols = dot(cumul, eye, (0, 0), HIGHEST)
    meta[me] = jnp.zeros(meta.shape[1:], F32)
    meta[me, 0:1, 0:heads] = cum_cols[tokens - 1 : tokens, :]
    meta[me, 1:2, :] = segs_row
    meta[me, 2:3, :] = jnp.broadcast_to(last_seg, (1, tokens))
    for w in loads[6:]:
        w.wait()
    pl.semaphore_wait(barrier, n_seq + n_head - 2)

    def rim_copies(target):
        tail = pl.ds(tokens - RIM, RIM)
        return [
            pltpu.make_async_remote_copy(
                src.at[tail, :], dst, rim_sem.at[0, i], rim_sem.at[1, i], device_id=at_seq(target), device_id_type=MESH
            )
            for i, (src, dst) in enumerate(((inner_ref, rim_inner), (groups_ref, rim_groups)))
        ]

    def meta_copy(slot, other):
        return pltpu.make_async_remote_copy(
            meta.at[slot], meta.at[slot], meta_ss.at[other], meta_rs.at[slot], device_id=at_seq(other), device_id_type=MESH
        )

    def kv_copy(slot, other):
        return pltpu.make_async_remote_copy(
            kv.at[slot, core],
            kv.at[slot, core],
            kv_ss.at[other],
            kv_rs.at[slot],
            device_id=at_seq(other),
            device_id_type=MESH,
        )

    def kv_share(slot):
        return pltpu.make_async_remote_copy(
            kv.at[slot, core],
            kv.at[slot, core],
            share_ss.at[slot],
            share_rs.at[slot],
            device_id=at_head(sibling),
            device_id_type=MESH,
        )

    following = lax.min(me + 1, n_seq - 1)
    previous = lax.max(me - 1, 0)

    @pl.when(me < n_seq - 1)
    def _():
        for c in rim_copies(following):
            c.start()

    def send_meta(d, _):
        meta_copy(me, (me + d) % n_seq).start()
        return 0

    lax.fori_loop(1, n_seq, send_meta, 0)

    def send_kv(k, _):
        kv_copy(me, k).start()
        return 0

    lax.fori_loop(me + 1, n_seq, send_kv, 0)

    pad_inner[RIM:, :] = inner_ref[...].astype(F32)
    pad_groups[RIM:, :] = groups_ref[...].astype(F32)

    def wait_meta(d, _):
        k = (me + d) % n_seq
        meta_copy(k, k).wait_recv()
        return 0

    lax.fori_loop(1, n_seq, wait_meta, 0)

    @pl.when(me > 0)
    def _():
        for c in rim_copies(previous):
            c.wait_recv()

    @pl.when(me == 0)
    def _():
        rim_inner[...] = jnp.zeros_like(rim_inner)
        rim_groups[...] = jnp.zeros_like(rim_groups)

    pad_inner[0:RIM, :] = rim_inner[...].astype(F32)
    pad_groups[0:RIM, :] = rim_groups[...].astype(F32)

    taps = taps_inner_ref.shape[0]
    prev_last = meta[previous, 2:3, 0:1]
    prev_segs = meta[previous, 1:2, :]
    token_col = iota((tokens, 1), 0)
    keeps = []
    for k in range(taps - 1):
        back = taps - 1 - k
        own = jnp.sum(
            jnp.where(row_t - back == col_t, jnp.broadcast_to(segs_row, (tokens, tokens)), 0.0), 1, keepdims=True
        )
        before = jnp.sum(
            jnp.where(row_t - back + tokens == col_t, jnp.broadcast_to(prev_segs, (tokens, tokens)), 0.0),
            1,
            keepdims=True,
        )
        keeps.append(jnp.where(token_col >= back, own, before) == segs_col)

    def conv(pad, weight_ref, out):
        for c in range(0, out.shape[1], LANES):
            cols = slice(c, c + LANES)
            acc = jnp.zeros((tokens, LANES), F32)
            for k in range(taps):
                first = RIM - (taps - 1) + k
                term = weight_ref[k : k + 1, cols] * pad[first : first + tokens, cols]
                acc = acc + (jnp.where(keeps[k], term, 0.0) if k < taps - 1 else term)
            out[:, cols] = jax.nn.silu(acc).astype(BF16)

    conv(pad_groups, taps_groups_ref, conv_bc)
    conv(pad_inner, taps_inner_ref, conv_x)

    read_b = conv_bc[:, :STATE_SIZE]
    read_c = conv_bc[:, STATE_SIZE:]
    in_last = segs_col == last_seg
    tail = jnp.where(in_last, jnp.exp(total_row - cumx[...]), 0.0)
    weighted = (tail * stepx * conv_x[...].astype(F32)).astype(BF16)
    state[...] = dot(read_b, weighted, (0, 0))

    partner = me + 1 - 2 * side
    upper = lax.min(me + 2, n_seq - 1)
    lower = lax.max(me - 2, 0)

    def part(which, c):
        return pl.ds(pl.multiple_of(which * half + c * LANES, LANES), LANES)

    def hop(src, dst, ss, rs, c, target):
        return pltpu.make_async_remote_copy(
            src.at[c], dst.at[c], ss.at[c], rs.at[c], device_id=at_seq(target), device_id_type=MESH
        )

    for c in range(chunks):
        s_send[c] = state[:, part(1 - side, c)].astype(BF16)
        hop(s_send, s_recv, s_ss, s_rs, c, partner).start()

    def c_copy():
        return pltpu.make_async_remote_copy(
            conv_bc.at[:, pl.ds(STATE_SIZE, STATE_SIZE)],
            partner_c,
            c_ss.at[0],
            c_rs.at[0],
            device_id=at_seq(partner),
            device_id_type=MESH,
        )

    c_copy().start()

    crossing = dot(read_c, read_b, (1, 1))
    live = (jnp.broadcast_to(segs_row, (tokens, tokens)) == segs_col) & (row_t >= col_t)
    left = iota((tokens, LANES), 1) < HEAD_CHANNELS
    for p in range(pairs):
        got = []
        for h in (2 * p, 2 * p + 1):
            decays = jnp.exp(jnp.where(live, cum_cols[:, h : h + 1] - cumul[h : h + 1, :], -jnp.inf))
            mixing = (crossing * decays * steps[h : h + 1, :]).astype(BF16)
            got.append(dot(mixing, conv_x[:, p * LANES : (p + 1) * LANES], (1, 0)))
        y_ref[:, p * LANES : (p + 1) * LANES] = jnp.where(left, got[0], got[1])

    scale = 1.0 / math.sqrt(HD)
    queries = jnp.concatenate([query_ref[:, h * HD : (h + 1) * HD] for h in range(heads_here)], axis=0)
    rows = heads_here * tokens
    segs_rows = jnp.concatenate([segs_col] * heads_here, axis=0)
    token_rows = jnp.concatenate([token_col] * heads_here, axis=0)

    def share(d, _):
        kv_copy(me - d, me).wait_recv()
        kv_share(me - d).start()
        return 0

    lax.fori_loop(1, me + 1, share, 0)

    def attend(d, carry):
        top, total, summed = carry
        k = me - d

        @pl.when(d > 0)
        def _():
            kv_share(k).wait_recv()

        scores = dot(queries, kv[k, 0], (1, 1)) * scale
        allowed = (meta[k, 1:2, :] == segs_rows) & (
            iota((rows, tokens), 1) + (k - me) * tokens <= token_rows
        )
        scores = jnp.where(allowed, scores, -jnp.inf)
        new_top = jnp.maximum(top, jnp.max(scores, axis=1, keepdims=True))
        rescale = jnp.exp(top - new_top)
        w = jnp.exp(scores - new_top)
        total = total * rescale + jnp.sum(w, axis=1, keepdims=True)
        summed = summed * rescale + dot(w.astype(BF16), kv[k, 1], (1, 0))
        return new_top, total, summed

    top, total, summed = lax.fori_loop(
        0,
        me + 1,
        attend,
        (jnp.full((rows, 1), -1e30, F32), jnp.zeros((rows, 1), F32), jnp.zeros((rows, HD), F32)),
    )
    attended = (summed / total).astype(BF16)
    for h in range(heads_here):
        both[:, channels + h * HD : channels + (h + 1) * HD] = attended[h * tokens : (h + 1) * tokens]

    @pl.when(pair == 0)
    def _():
        e_recv[...] = jnp.zeros_like(e_recv)

    first, second = pair * 2, pair * 2 + 1
    seg_before = meta[lax.max(first - 1, 0), 2:3, 0:1]
    seg_first = meta[first, 2:3, 0:1]
    seg_second = meta[second, 2:3, 0:1]
    through[0:1, :] = jnp.where(
        seg_first == seg_before, jnp.exp(dot(meta[first, 0:1, 0:heads], spread, (1, 0), HIGHEST)), 0.0
    )
    through[1:2, :] = jnp.where(
        seg_second == seg_first, jnp.exp(dot(meta[second, 0:1, 0:heads], spread, (1, 0), HIGHEST)), 0.0
    )
    c_copy().wait_recv()
    on_left = side == 0
    for c in range(chunks):
        cols = part(side, c)
        through_first = through[0:1, cols]
        through_second = through[1:2, cols]
        hop(s_send, s_recv, s_ss, s_rs, c, partner).wait_recv()
        own, others = state[:, cols], s_recv[c].astype(F32)

        @pl.when(pair > 0)
        def _():
            hop(e_send, e_recv, e_ss, e_rs, c, lower).wait_recv()

        enter_first = e_recv[c].astype(F32)
        enter_second = through_first * enter_first + jnp.where(on_left, own, others)

        @pl.when(pair < last_pair)
        def _():
            e_send[c] = (through_second * enter_second + jnp.where(on_left, others, own)).astype(BF16)
            hop(e_send, e_recv, e_ss, e_rs, c, upper).start()

        theirs = jnp.where(on_left, enter_second, enter_first).astype(BF16)
        f_send[c] = dot(partner_c[...], theirs, (1, 0)).astype(BF16)
        hop(f_send, f_recv, f_ss, f_rs, c, partner).start()
        ours = jnp.where(on_left, enter_first, enter_second).astype(BF16)
        carried_ref[:, cols] = dot(read_c, ours, (1, 0))

    for c in range(chunks):
        hop(f_send, f_recv, f_ss, f_rs, c, partner).wait_recv()
        carried_ref[:, part(1 - side, c)] = f_recv[c].astype(F32)

    joined = segs_col == prev_last
    gain_row = gain_ref[...].reshape(1, channels)
    same_head = (iota((LANES, LANES), 0) // HEAD_CHANNELS == iota((LANES, LANES), 1) // HEAD_CHANNELS).astype(F32)
    for p in range(pairs):
        cols = slice(p * LANES, (p + 1) * LANES)
        carried = carried_ref[:, cols]
        y = y_ref[:, cols] + jnp.where(joined, jnp.exp(cumx[:, cols]), 0.0) * carried
        gated = y * jax.nn.silu(gate_ref[:, cols].astype(F32))
        mean_square = dot(gated * gated, same_head, (1, 0), HIGHEST) * (1.0 / HEAD_CHANNELS)
        both[:, cols] = (gated * lax.rsqrt(mean_square + 1e-05) * gain_row[:, cols]).astype(BF16)

    for w in weights:
        w.wait()
    width = out_ref.shape[1]

    def product(j):
        cols = pl.ds(pl.multiple_of(j * width, LANES), width)
        return dot(both[:, :channels], mproj[:, cols], (1, 0)) + dot(both[:, channels:], aproj[:, cols], (1, 0))

    def rs_copy(i, target):
        return pltpu.make_async_remote_copy(
            rs_send.at[i], rs_recv.at[i], rs_ss.at[i], rs_rs.at[i], device_id=at_head(target), device_id_type=MESH
        )

    to_pair, to_sibling, to_opposite = rs_copy(0, sibling), rs_copy(1, sibling), rs_copy(2, opposite)
    rs_send[0] = product(opposite_sibling).astype(BF16)
    to_pair.start()
    rs_send[1] = product(sibling).astype(BF16)
    to_sibling.start()
    away = product(opposite)
    to_pair.wait_recv()
    rs_send[2] = (away + rs_recv[0].astype(F32)).astype(BF16)
    to_opposite.start()
    result = product(mine)
    to_sibling.wait_recv()
    result = result + rs_recv[1].astype(F32)
    to_opposite.wait_recv()
    out_ref[...] = (result + rs_recv[2].astype(F32)).astype(BF16)

    for copy in (to_pair, to_sibling, to_opposite, c_copy()):
        copy.wait_send()

    def sent_share(d, _):
        kv_share(me - d).wait_send()
        return 0

    lax.fori_loop(1, me + 1, sent_share, 0)

    @pl.when(me < n_seq - 1)
    def _():
        for c in rim_copies(following):
            c.wait_send()

    def sent_meta(d, _):
        meta_copy(me, (me + d) % n_seq).wait_send()
        return 0

    lax.fori_loop(1, n_seq, sent_meta, 0)

    def sent_kv(k, _):
        kv_copy(me, k).wait_send()
        return 0

    lax.fori_loop(me + 1, n_seq, sent_kv, 0)
    for c in range(chunks):
        hop(s_send, s_recv, s_ss, s_rs, c, partner).wait_send()
        hop(f_send, f_recv, f_ss, f_rs, c, partner).wait_send()

        @pl.when(pair < last_pair)
        def _():
            hop(e_send, e_recv, e_ss, e_rs, c, upper).wait_send()


def shards(n_seq, n_head, *arrays):
    (inner, groups, gate, step, bias, decay, taps_i, taps_g, gain, query, key, value, segs, mproj, aproj) = arrays
    tokens, channels = inner.shape
    out_width = mproj.shape[1] // n_head
    chunks = channels // 2 // LANES
    hops = (chunks, STATE_SIZE, LANES)
    vmem = pl.BlockSpec(memory_space=pltpu.VMEM)
    hbm = pl.BlockSpec(memory_space=pltpu.HBM)
    dma = pltpu.SemaphoreType.DMA
    scratch = [
        *[pltpu.VMEM(a.shape, a.dtype) for a in arrays[:13]],
        pltpu.VMEM(mproj.shape, BF16),
        pltpu.VMEM(aproj.shape, BF16),
        pltpu.VMEM((tokens + RIM, channels), F32),
        pltpu.VMEM((tokens + RIM, groups.shape[1]), F32),
        pltpu.VMEM((RIM, channels), BF16),
        pltpu.VMEM((RIM, groups.shape[1]), BF16),
        pltpu.VMEM((n_seq, 8, tokens), F32),
        pltpu.VMEM((n_seq, 2, tokens, HD), BF16),
        pltpu.VMEM((tokens, channels), BF16),
        pltpu.VMEM((tokens, groups.shape[1]), BF16),
        pltpu.VMEM((tokens, channels), F32),
        pltpu.VMEM((tokens, channels), F32),
        pltpu.VMEM((STATE_SIZE, channels), F32),
        *[pltpu.VMEM(hops, BF16) for _ in range(4)],
        *[pltpu.VMEM((chunks, tokens, LANES), BF16) for _ in range(2)],
        pltpu.VMEM((tokens, STATE_SIZE), BF16),
        pltpu.VMEM((tokens, channels), F32),
        pltpu.VMEM((8, channels), F32),
        pltpu.VMEM((tokens, channels + query.shape[1]), BF16),
        pltpu.VMEM((n_head - 1, tokens, out_width), BF16),
        pltpu.VMEM((n_head - 1, tokens, out_width), BF16),
        dma((13,)),
        dma((2,)),
        dma((2, 2)),
        dma((n_seq,)),
        dma((n_seq,)),
        dma((n_seq,)),
        dma((n_seq,)),
        dma((n_seq,)),
        dma((n_seq,)),
        dma((1,)),
        dma((1,)),
        *[dma((chunks,)) for _ in range(6)],
        dma((n_head - 1,)),
        dma((n_head - 1,)),
    ]
    return pl.pallas_call(
        functools.partial(kernel, n_seq, n_head),
        out_shape=jax.ShapeDtypeStruct((tokens, out_width), BF16),
        in_specs=[hbm] * 15,
        out_specs=vmem,
        scratch_shapes=scratch,
        compiler_params=pltpu.CompilerParams(
            collective_id=0, has_side_effects=True, vmem_limit_bytes=48 * 2**20
        ),
        name="mixer",
    )(
        inner,
        groups,
        gate,
        step,
        bias,
        decay,
        taps_i,
        taps_g,
        gain,
        query,
        key,
        value,
        segs,
        mproj,
        aproj,
    )


def solution(mesh):
    placed = (
        P("seq", "head"),
        P("seq", None),
        P("seq", "head"),
        P("head", "seq"),
        P("head"),
        P("head"),
        P(None, "head"),
        P(),
        P("head"),
        P("seq", "head"),
        P("seq", None),
        P("seq", None),
        P("seq"),
        P("head", None),
        P("head", None),
    )
    return jax.shard_map(
        functools.partial(shards, mesh.shape["seq"], mesh.shape["head"]),
        mesh=mesh,
        in_specs=placed,
        out_specs=P("seq", "head"),
        check_vma=False,
    )
```

```python
import functools
import math

import jax
import jax.numpy as jnp
from jax import lax
from jax.experimental import pallas as pl
from jax.experimental.pallas import tpu as pltpu
from jax.sharding import PartitionSpec as P

HEAD_CHANNELS = 64
STATE_SIZE = 256
QH = 8
KVH = 2
HD = 128
LANES = 128
RIM = 16
F32 = jnp.float32
BF16 = jnp.bfloat16
MESH = pl.DeviceIdType.MESH
HIGHEST = lax.Precision.HIGHEST


def dot(a, b, contract, precision=None):
    return lax.dot_general(
        a, b, ((contract[:1], contract[1:]), ((), ())), precision=precision, preferred_element_type=F32
    )


def iota(shape, axis):
    return lax.broadcasted_iota(jnp.int32, shape, axis)


def column(row):
    n = row.shape[1]
    eye = iota((n, n), 0) == iota((n, n), 1)
    return jnp.sum(jnp.where(eye, jnp.broadcast_to(row, (n, n)), 0.0), axis=1, keepdims=True)


def kernel(
    n_seq,
    n_head,
    inner_hbm,
    groups_hbm,
    gate_hbm,
    step_hbm,
    bias_hbm,
    decay_hbm,
    taps_inner_hbm,
    taps_groups_hbm,
    gain_hbm,
    query_hbm,
    key_hbm,
    value_hbm,
    segs_hbm,
    mamba_proj_hbm,
    attn_proj_hbm,
    out_ref,
    inner_ref,
    groups_ref,
    gate_ref,
    step_ref,
    bias_ref,
    decay_ref,
    taps_inner_ref,
    taps_groups_ref,
    gain_ref,
    query_ref,
    key_ref,
    value_ref,
    segs_ref,
    mproj,
    aproj,
    pad_inner,
    pad_groups,
    rim_inner,
    rim_groups,
    meta,
    kv,
    conv_x,
    conv_bc,
    cumx,
    y_ref,
    state,
    s_send,
    s_recv,
    e_send,
    e_recv,
    f_send,
    f_recv,
    partner_c,
    entering,
    through,
    both,
    rs_send,
    rs_recv,
    load_sem,
    weight_sem,
    rim_sem,
    meta_ss,
    meta_rs,
    kv_ss,
    kv_rs,
    share_ss,
    share_rs,
    c_ss,
    c_rs,
    s_ss,
    s_rs,
    e_ss,
    e_rs,
    f_ss,
    f_rs,
    rs_ss,
    rs_rs,
):
    tokens, channels = inner_ref.shape
    heads = step_ref.shape[0]
    half = channels // 2
    chunks = half // LANES
    pairs = channels // LANES
    me = lax.axis_index("seq")
    mine = lax.axis_index("head")
    pair, side = me // 2, me % 2
    last_pair = n_seq // 2 - 1
    heads_here = query_ref.shape[1] // HD
    core = mine % 2
    sibling = mine + 1 - 2 * core
    opposite = (mine + 2) % n_head
    opposite_sibling = (sibling + 2) % n_head

    def at_seq(s):
        return (s, mine)

    def at_head(h):
        return (me, h)

    weights = [
        pltpu.make_async_copy(mamba_proj_hbm, mproj, weight_sem.at[0]),
        pltpu.make_async_copy(attn_proj_hbm, aproj, weight_sem.at[1]),
    ]
    loads = [
        pltpu.make_async_copy(src, dst, load_sem.at[i])
        for i, (src, dst) in enumerate(
            (
                (step_hbm, step_ref),
                (bias_hbm, bias_ref),
                (decay_hbm, decay_ref),
                (segs_hbm, segs_ref),
                (key_hbm, key_ref),
                (value_hbm, value_ref),
                (inner_hbm, inner_ref),
                (groups_hbm, groups_ref),
                (taps_inner_hbm, taps_inner_ref),
                (taps_groups_hbm, taps_groups_ref),
                (query_hbm, query_ref),
                (gate_hbm, gate_ref),
                (gain_hbm, gain_ref),
            )
        )
    ]
    for w in loads + weights:
        w.start()

    barrier = pltpu.get_barrier_semaphore()
    for d in range(1, n_seq):
        pl.semaphore_signal(barrier, inc=1, device_id=at_seq((me + d) % n_seq), device_id_type=MESH)
    for d in range(1, n_head):
        pl.semaphore_signal(barrier, inc=1, device_id=at_head((mine + d) % n_head), device_id_type=MESH)

    for w in loads[:6]:
        w.wait()
    kv_head = mine * heads_here // (QH // KVH)
    kv_cols = pl.ds(pl.multiple_of(kv_head * HD, HD), HD)
    kv[me, 0] = key_ref[:, kv_cols]
    kv[me, 1] = value_ref[:, kv_cols]

    raw = step_ref[...] + column(bias_ref[...].reshape(1, heads))
    steps = jnp.maximum(raw, 0.0) + jnp.log1p(jnp.exp(-jnp.abs(raw)))
    rates = jnp.exp(column(decay_ref[...].reshape(1, heads)))
    row_t, col_t = iota((tokens, tokens), 0), iota((tokens, tokens), 1)
    upto = (row_t <= col_t).astype(F32)
    cumul = dot(-steps * rates, upto, (1, 0), HIGHEST)
    spread = (iota((heads, channels), 1) // HEAD_CHANNELS == iota((heads, channels), 0)).astype(F32)
    cumx[...] = dot(cumul, spread, (0, 0), HIGHEST)
    stepx = dot(steps, spread, (0, 0), HIGHEST)
    total_row = cumx[tokens - 1 : tokens, :]
    segs_row = segs_ref[...].reshape(1, tokens).astype(F32)
    segs_col = column(segs_row)
    last_seg = segs_row[:, tokens - 1 : tokens]
    eye = (iota((heads, heads), 0) == iota((heads, heads), 1)).astype(F32)
    cum_cols = dot(cumul, eye, (0, 0), HIGHEST)
    meta[me] = jnp.zeros(meta.shape[1:], F32)
    meta[me, 0:1, 0:heads] = cum_cols[tokens - 1 : tokens, :]
    meta[me, 1:2, :] = segs_row
    meta[me, 2:3, :] = jnp.broadcast_to(last_seg, (1, tokens))
    for w in loads[6:]:
        w.wait()
    pl.semaphore_wait(barrier, n_seq + n_head - 2)

    def rim_copies(target):
        tail = pl.ds(tokens - RIM, RIM)
        return [
            pltpu.make_async_remote_copy(
                src.at[tail, :], dst, rim_sem.at[0, i], rim_sem.at[1, i], device_id=at_seq(target), device_id_type=MESH
            )
            for i, (src, dst) in enumerate(((inner_ref, rim_inner), (groups_ref, rim_groups)))
        ]

    def meta_copy(slot, other):
        return pltpu.make_async_remote_copy(
            meta.at[slot], meta.at[slot], meta_ss.at[other], meta_rs.at[slot], device_id=at_seq(other), device_id_type=MESH
        )

    def kv_copy(slot, other):
        return pltpu.make_async_remote_copy(
            kv.at[slot, core],
            kv.at[slot, core],
            kv_ss.at[other],
            kv_rs.at[slot],
            device_id=at_seq(other),
            device_id_type=MESH,
        )

    def kv_share(slot):
        return pltpu.make_async_remote_copy(
            kv.at[slot, core],
            kv.at[slot, core],
            share_ss.at[slot],
            share_rs.at[slot],
            device_id=at_head(sibling),
            device_id_type=MESH,
        )

    following = lax.min(me + 1, n_seq - 1)
    previous = lax.max(me - 1, 0)

    @pl.when(me < n_seq - 1)
    def _():
        for c in rim_copies(following):
            c.start()

    def send_meta(d, _):
        meta_copy(me, (me + d) % n_seq).start()
        return 0

    lax.fori_loop(1, n_seq, send_meta, 0)

    def send_kv(k, _):
        kv_copy(me, k).start()
        return 0

    lax.fori_loop(me + 1, n_seq, send_kv, 0)

    pad_inner[RIM:, :] = inner_ref[...].astype(F32)
    pad_groups[RIM:, :] = groups_ref[...].astype(F32)

    @pl.when(me > 0)
    def _():
        meta_copy(previous, previous).wait_recv()
        for c in rim_copies(previous):
            c.wait_recv()

    @pl.when(me == 0)
    def _():
        rim_inner[...] = jnp.zeros_like(rim_inner)
        rim_groups[...] = jnp.zeros_like(rim_groups)

    pad_inner[0:RIM, :] = rim_inner[...].astype(F32)
    pad_groups[0:RIM, :] = rim_groups[...].astype(F32)

    taps = taps_inner_ref.shape[0]
    prev_last = meta[previous, 2:3, 0:1]
    prev_segs = meta[previous, 1:2, :]
    token_col = iota((tokens, 1), 0)
    keeps = []
    for k in range(taps - 1):
        back = taps - 1 - k
        own = jnp.sum(
            jnp.where(row_t - back == col_t, jnp.broadcast_to(segs_row, (tokens, tokens)), 0.0), 1, keepdims=True
        )
        before = jnp.sum(
            jnp.where(row_t - back + tokens == col_t, jnp.broadcast_to(prev_segs, (tokens, tokens)), 0.0),
            1,
            keepdims=True,
        )
        keeps.append(jnp.where(token_col >= back, own, before) == segs_col)

    def conv(pad, weight_ref, out):
        for c in range(0, out.shape[1], LANES):
            cols = slice(c, c + LANES)
            acc = jnp.zeros((tokens, LANES), F32)
            for k in range(taps):
                first = RIM - (taps - 1) + k
                term = weight_ref[k : k + 1, cols] * pad[first : first + tokens, cols]
                acc = acc + (jnp.where(keeps[k], term, 0.0) if k < taps - 1 else term)
            out[:, cols] = jax.nn.silu(acc).astype(BF16)

    conv(pad_groups, taps_groups_ref, conv_bc)
    conv(pad_inner, taps_inner_ref, conv_x)

    read_b = conv_bc[:, :STATE_SIZE]
    read_c = conv_bc[:, STATE_SIZE:]
    in_last = segs_col == last_seg
    tail = jnp.where(in_last, jnp.exp(total_row - cumx[...]), 0.0)
    weighted = (tail * stepx * conv_x[...].astype(F32)).astype(BF16)
    state[...] = dot(read_b, weighted, (0, 0))

    partner = me + 1 - 2 * side
    upper = lax.min(me + 2, n_seq - 1)
    lower = lax.max(me - 2, 0)

    def part(which, c):
        return pl.ds(pl.multiple_of(which * half + c * LANES, LANES), LANES)

    def hop(src, dst, ss, rs, c, target):
        return pltpu.make_async_remote_copy(
            src.at[c], dst.at[c], ss.at[c], rs.at[c], device_id=at_seq(target), device_id_type=MESH
        )

    for c in range(chunks):
        s_send[c] = state[:, part(1 - side, c)].astype(BF16)
        hop(s_send, s_recv, s_ss, s_rs, c, partner).start()

    def c_copy():
        return pltpu.make_async_remote_copy(
            conv_bc.at[:, pl.ds(STATE_SIZE, STATE_SIZE)],
            partner_c,
            c_ss.at[0],
            c_rs.at[0],
            device_id=at_seq(partner),
            device_id_type=MESH,
        )

    c_copy().start()

    def wait_meta(d, _):
        k = (me + d) % n_seq
        meta_copy(k, k).wait_recv()
        return 0

    lax.fori_loop(1, n_seq - 1, wait_meta, 0)

    @pl.when(me == 0)
    def _():
        meta_copy(n_seq - 1, n_seq - 1).wait_recv()

    crossing = dot(read_c, read_b, (1, 1))
    live = (jnp.broadcast_to(segs_row, (tokens, tokens)) == segs_col) & (row_t >= col_t)
    left = iota((tokens, LANES), 1) < HEAD_CHANNELS
    for p in range(pairs):
        got = []
        for h in (2 * p, 2 * p + 1):
            decays = jnp.exp(jnp.where(live, cum_cols[:, h : h + 1] - cumul[h : h + 1, :], -jnp.inf))
            mixing = (crossing * decays * steps[h : h + 1, :]).astype(BF16)
            got.append(dot(mixing, conv_x[:, p * LANES : (p + 1) * LANES], (1, 0)))
        y_ref[:, p * LANES : (p + 1) * LANES] = jnp.where(left, got[0], got[1])

    scale = 1.0 / math.sqrt(HD)
    queries = jnp.concatenate([query_ref[:, h * HD : (h + 1) * HD] for h in range(heads_here)], axis=0)
    rows = heads_here * tokens
    segs_rows = jnp.concatenate([segs_col] * heads_here, axis=0)
    token_rows = jnp.concatenate([token_col] * heads_here, axis=0)

    def share(d, _):
        kv_copy(me - d, me).wait_recv()
        kv_share(me - d).start()
        return 0

    def attend(d, carry):
        top, total, summed = carry
        k = me - d

        @pl.when(d > 0)
        def _():
            kv_share(k).wait_recv()

        scores = dot(queries, kv[k, 0], (1, 1)) * scale
        allowed = (meta[k, 1:2, :] == segs_rows) & (
            iota((rows, tokens), 1) + (k - me) * tokens <= token_rows
        )
        scores = jnp.where(allowed, scores, -jnp.inf)
        new_top = jnp.maximum(top, jnp.max(scores, axis=1, keepdims=True))
        rescale = jnp.exp(top - new_top)
        w = jnp.exp(scores - new_top)
        total = total * rescale + jnp.sum(w, axis=1, keepdims=True)
        summed = summed * rescale + dot(w.astype(BF16), kv[k, 1], (1, 0))
        return new_top, total, summed

    def attention():
        lax.fori_loop(1, me + 1, share, 0)
        top, total, summed = lax.fori_loop(
            0,
            me + 1,
            attend,
            (jnp.full((rows, 1), -1e30, F32), jnp.zeros((rows, 1), F32), jnp.zeros((rows, HD), F32)),
        )
        attended = (summed / total).astype(BF16)
        for h in range(heads_here):
            both[:, channels + h * HD : channels + (h + 1) * HD] = attended[h * tokens : (h + 1) * tokens]

    pl.when(me >= n_seq // 2)(attention)

    @pl.when(pair == 0)
    def _():
        e_recv[...] = jnp.zeros_like(e_recv)

    first, second = pair * 2, pair * 2 + 1
    seg_before = meta[lax.max(first - 1, 0), 2:3, 0:1]
    seg_first = meta[first, 2:3, 0:1]
    seg_second = meta[second, 2:3, 0:1]
    through[0:1, :] = jnp.where(
        seg_first == seg_before, jnp.exp(dot(meta[first, 0:1, 0:heads], spread, (1, 0), HIGHEST)), 0.0
    )
    through[1:2, :] = jnp.where(
        seg_second == seg_first, jnp.exp(dot(meta[second, 0:1, 0:heads], spread, (1, 0), HIGHEST)), 0.0
    )
    through[2:3, :] = gain_ref[...].reshape(1, channels)
    c_copy().wait_recv()
    on_left = side == 0
    for c in range(chunks):
        cols = part(side, c)
        through_first = through[0:1, cols]
        through_second = through[1:2, cols]
        hop(s_send, s_recv, s_ss, s_rs, c, partner).wait_recv()
        own, others = state[:, cols], s_recv[c].astype(F32)

        @pl.when(pair > 0)
        def _():
            hop(e_send, e_recv, e_ss, e_rs, c, lower).wait_recv()

        enter_first = e_recv[c].astype(F32)
        enter_second = through_first * enter_first + jnp.where(on_left, own, others)

        @pl.when(pair < last_pair)
        def _():
            e_send[c] = (through_second * enter_second + jnp.where(on_left, others, own)).astype(BF16)
            hop(e_send, e_recv, e_ss, e_rs, c, upper).start()

        theirs = jnp.where(on_left, enter_second, enter_first).astype(BF16)
        f_send[c] = dot(partner_c[...], theirs, (1, 0)).astype(BF16)
        hop(f_send, f_recv, f_ss, f_rs, c, partner).start()
        entering[c] = jnp.where(on_left, enter_first, enter_second).astype(BF16)

    joined = segs_col == prev_last
    same_head = (iota((LANES, LANES), 0) // HEAD_CHANNELS == iota((LANES, LANES), 1) // HEAD_CHANNELS).astype(F32)

    def norm(cols, carried):
        y = y_ref[:, cols] + jnp.where(joined, jnp.exp(cumx[:, cols]), 0.0) * carried
        gated = y * jax.nn.silu(gate_ref[:, cols].astype(F32))
        mean_square = dot(gated * gated, same_head, (1, 0), HIGHEST) * (1.0 / HEAD_CHANNELS)
        both[:, cols] = (gated * lax.rsqrt(mean_square + 1e-05) * through[2:3, cols]).astype(BF16)

    pl.when(me < n_seq // 2)(attention)
    for c in range(chunks):
        norm(part(side, c), dot(read_c, entering[c], (1, 0)))
    for c in range(chunks):
        hop(f_send, f_recv, f_ss, f_rs, c, partner).wait_recv()
        norm(part(1 - side, c), f_recv[c].astype(F32))

    for w in weights:
        w.wait()
    width = out_ref.shape[1]

    def product(j):
        cols = pl.ds(pl.multiple_of(j * width, LANES), width)
        return dot(both[:, :channels], mproj[:, cols], (1, 0)) + dot(both[:, channels:], aproj[:, cols], (1, 0))

    def rs_copy(i, target):
        return pltpu.make_async_remote_copy(
            rs_send.at[i], rs_recv.at[i], rs_ss.at[i], rs_rs.at[i], device_id=at_head(target), device_id_type=MESH
        )

    to_pair, to_sibling, to_opposite = rs_copy(0, sibling), rs_copy(1, sibling), rs_copy(2, opposite)
    rs_send[0] = product(opposite_sibling).astype(BF16)
    to_pair.start()
    rs_send[1] = product(sibling).astype(BF16)
    to_sibling.start()
    away = product(opposite)
    to_pair.wait_recv()
    rs_send[2] = (away + rs_recv[0].astype(F32)).astype(BF16)
    to_opposite.start()
    result = product(mine)
    to_sibling.wait_recv()
    result = result + rs_recv[1].astype(F32)
    to_opposite.wait_recv()
    out_ref[...] = (result + rs_recv[2].astype(F32)).astype(BF16)

    for copy in (to_pair, to_sibling, to_opposite, c_copy()):
        copy.wait_send()

    def sent_share(d, _):
        kv_share(me - d).wait_send()
        return 0

    lax.fori_loop(1, me + 1, sent_share, 0)

    @pl.when(me < n_seq - 1)
    def _():
        for c in rim_copies(following):
            c.wait_send()

    def sent_meta(d, _):
        meta_copy(me, (me + d) % n_seq).wait_send()
        return 0

    lax.fori_loop(1, n_seq, sent_meta, 0)

    def sent_kv(k, _):
        kv_copy(me, k).wait_send()
        return 0

    lax.fori_loop(me + 1, n_seq, sent_kv, 0)
    for c in range(chunks):
        hop(s_send, s_recv, s_ss, s_rs, c, partner).wait_send()
        hop(f_send, f_recv, f_ss, f_rs, c, partner).wait_send()

        @pl.when(pair < last_pair)
        def _():
            hop(e_send, e_recv, e_ss, e_rs, c, upper).wait_send()


def shards(n_seq, n_head, *arrays):
    (inner, groups, gate, step, bias, decay, taps_i, taps_g, gain, query, key, value, segs, mproj, aproj) = arrays
    tokens, channels = inner.shape
    out_width = mproj.shape[1] // n_head
    chunks = channels // 2 // LANES
    hops = (chunks, STATE_SIZE, LANES)
    vmem = pl.BlockSpec(memory_space=pltpu.VMEM)
    hbm = pl.BlockSpec(memory_space=pltpu.HBM)
    dma = pltpu.SemaphoreType.DMA
    scratch = [
        *[pltpu.VMEM(a.shape, a.dtype) for a in arrays[:13]],
        pltpu.VMEM(mproj.shape, BF16),
        pltpu.VMEM(aproj.shape, BF16),
        pltpu.VMEM((tokens + RIM, channels), F32),
        pltpu.VMEM((tokens + RIM, groups.shape[1]), F32),
        pltpu.VMEM((RIM, channels), BF16),
        pltpu.VMEM((RIM, groups.shape[1]), BF16),
        pltpu.VMEM((n_seq, 8, tokens), F32),
        pltpu.VMEM((n_seq, 2, tokens, HD), BF16),
        pltpu.VMEM((tokens, channels), BF16),
        pltpu.VMEM((tokens, groups.shape[1]), BF16),
        pltpu.VMEM((tokens, channels), F32),
        pltpu.VMEM((tokens, channels), F32),
        pltpu.VMEM((STATE_SIZE, channels), F32),
        *[pltpu.VMEM(hops, BF16) for _ in range(4)],
        *[pltpu.VMEM((chunks, tokens, LANES), BF16) for _ in range(2)],
        pltpu.VMEM((tokens, STATE_SIZE), BF16),
        pltpu.VMEM(hops, BF16),
        pltpu.VMEM((8, channels), F32),
        pltpu.VMEM((tokens, channels + query.shape[1]), BF16),
        pltpu.VMEM((n_head - 1, tokens, out_width), BF16),
        pltpu.VMEM((n_head - 1, tokens, out_width), BF16),
        dma((13,)),
        dma((2,)),
        dma((2, 2)),
        dma((n_seq,)),
        dma((n_seq,)),
        dma((n_seq,)),
        dma((n_seq,)),
        dma((n_seq,)),
        dma((n_seq,)),
        dma((1,)),
        dma((1,)),
        *[dma((chunks,)) for _ in range(6)],
        dma((n_head - 1,)),
        dma((n_head - 1,)),
    ]
    return pl.pallas_call(
        functools.partial(kernel, n_seq, n_head),
        out_shape=jax.ShapeDtypeStruct((tokens, out_width), BF16),
        in_specs=[hbm] * 15,
        out_specs=vmem,
        scratch_shapes=scratch,
        compiler_params=pltpu.CompilerParams(
            collective_id=0, has_side_effects=True, vmem_limit_bytes=64 * 2**20
        ),
        name="mixer",
    )(
        inner,
        groups,
        gate,
        step,
        bias,
        decay,
        taps_i,
        taps_g,
        gain,
        query,
        key,
        value,
        segs,
        mproj,
        aproj,
    )


def solution(mesh):
    placed = (
        P("seq", "head"),
        P("seq", None),
        P("seq", "head"),
        P("head", "seq"),
        P("head"),
        P("head"),
        P(None, "head"),
        P(),
        P("head"),
        P("seq", "head"),
        P("seq", None),
        P("seq", None),
        P("seq"),
        P("head", None),
        P("head", None),
    )
    return jax.shard_map(
        functools.partial(shards, mesh.shape["seq"], mesh.shape["head"]),
        mesh=mesh,
        in_specs=placed,
        out_specs=P("seq", "head"),
        check_vma=False,
    )
```

```python
import functools
import math

import jax
import jax.numpy as jnp
from jax import lax
from jax.experimental import pallas as pl
from jax.experimental.pallas import tpu as pltpu
from jax.sharding import PartitionSpec as P

HEAD_CHANNELS = 64
STATE_SIZE = 256
QH = 8
KVH = 2
HD = 128
LANES = 128
RIM = 16
F32 = jnp.float32
BF16 = jnp.bfloat16
MESH = pl.DeviceIdType.MESH
HIGHEST = lax.Precision.HIGHEST


def dot(a, b, contract, precision=None):
    return lax.dot_general(
        a, b, ((contract[:1], contract[1:]), ((), ())), precision=precision, preferred_element_type=F32
    )


def iota(shape, axis):
    return lax.broadcasted_iota(jnp.int32, shape, axis)


def column(row):
    n = row.shape[1]
    eye = iota((n, n), 0) == iota((n, n), 1)
    return jnp.sum(jnp.where(eye, jnp.broadcast_to(row, (n, n)), 0.0), axis=1, keepdims=True)


def kernel(
    n_seq,
    n_head,
    inner_hbm,
    groups_hbm,
    gate_hbm,
    step_hbm,
    bias_hbm,
    decay_hbm,
    taps_inner_hbm,
    taps_groups_hbm,
    gain_hbm,
    query_hbm,
    key_hbm,
    value_hbm,
    segs_hbm,
    mamba_proj_hbm,
    attn_proj_hbm,
    out_ref,
    inner_ref,
    groups_ref,
    gate_ref,
    step_ref,
    bias_ref,
    decay_ref,
    taps_inner_ref,
    taps_groups_ref,
    gain_ref,
    query_ref,
    key_ref,
    value_ref,
    segs_ref,
    mproj,
    aproj,
    pad_inner,
    pad_groups,
    rim_inner,
    rim_groups,
    meta,
    kv,
    conv_x,
    conv_bc,
    cumx,
    y_ref,
    state,
    s_send,
    s_recv,
    e_send,
    e_recv,
    f_send,
    f_recv,
    partner_c,
    entering,
    through,
    both,
    rs_send,
    rs_recv,
    load_sem,
    weight_sem,
    rim_sem,
    meta_ss,
    meta_rs,
    kv_ss,
    kv_rs,
    share_ss,
    share_rs,
    c_ss,
    c_rs,
    s_ss,
    s_rs,
    e_ss,
    e_rs,
    f_ss,
    f_rs,
    rs_ss,
    rs_rs,
):
    tokens, channels = inner_ref.shape
    heads = step_ref.shape[0]
    half = channels // 2
    chunks = half // LANES
    pairs = channels // LANES
    me = lax.axis_index("seq")
    mine = lax.axis_index("head")
    pair, side = me // 2, me % 2
    last_pair = n_seq // 2 - 1
    heads_here = query_ref.shape[1] // HD
    core = mine % 2
    sibling = mine + 1 - 2 * core
    opposite = (mine + 2) % n_head
    opposite_sibling = (sibling + 2) % n_head

    def at_seq(s):
        return (s, mine)

    def at_head(h):
        return (me, h)

    weights = [
        pltpu.make_async_copy(mamba_proj_hbm, mproj, weight_sem.at[0]),
        pltpu.make_async_copy(attn_proj_hbm, aproj, weight_sem.at[1]),
    ]
    loads = [
        pltpu.make_async_copy(src, dst, load_sem.at[i])
        for i, (src, dst) in enumerate(
            (
                (step_hbm, step_ref),
                (bias_hbm, bias_ref),
                (decay_hbm, decay_ref),
                (segs_hbm, segs_ref),
                (key_hbm, key_ref),
                (value_hbm, value_ref),
                (inner_hbm, inner_ref),
                (groups_hbm, groups_ref),
                (taps_inner_hbm, taps_inner_ref),
                (taps_groups_hbm, taps_groups_ref),
                (query_hbm, query_ref),
                (gate_hbm, gate_ref),
                (gain_hbm, gain_ref),
            )
        )
    ]
    for w in loads + weights:
        w.start()

    barrier = pltpu.get_barrier_semaphore()
    for d in range(1, n_seq):
        pl.semaphore_signal(barrier, inc=1, device_id=at_seq((me + d) % n_seq), device_id_type=MESH)
    for d in range(1, n_head):
        pl.semaphore_signal(barrier, inc=1, device_id=at_head((mine + d) % n_head), device_id_type=MESH)

    for w in loads[:6]:
        w.wait()
    kv_head = mine * heads_here // (QH // KVH)
    kv_cols = pl.ds(pl.multiple_of(kv_head * HD, HD), HD)
    kv[me, 0] = key_ref[:, kv_cols]
    kv[me, 1] = value_ref[:, kv_cols]

    raw = step_ref[...] + column(bias_ref[...].reshape(1, heads))
    steps = jnp.maximum(raw, 0.0) + jnp.log1p(jnp.exp(-jnp.abs(raw)))
    rates = jnp.exp(column(decay_ref[...].reshape(1, heads)))
    row_t, col_t = iota((tokens, tokens), 0), iota((tokens, tokens), 1)
    upto = (row_t <= col_t).astype(F32)
    cumul = dot(-steps * rates, upto, (1, 0), HIGHEST)
    spread = (iota((heads, channels), 1) // HEAD_CHANNELS == iota((heads, channels), 0)).astype(F32)
    cumx[...] = dot(cumul, spread, (0, 0), HIGHEST)
    stepx = dot(steps, spread, (0, 0), HIGHEST)
    total_row = cumx[tokens - 1 : tokens, :]
    segs_row = segs_ref[...].reshape(1, tokens).astype(F32)
    segs_col = column(segs_row)
    last_seg = segs_row[:, tokens - 1 : tokens]
    eye = (iota((heads, heads), 0) == iota((heads, heads), 1)).astype(F32)
    cum_cols = dot(cumul, eye, (0, 0), HIGHEST)
    meta[me] = jnp.zeros(meta.shape[1:], F32)
    meta[me, 0:1, 0:heads] = cum_cols[tokens - 1 : tokens, :]
    meta[me, 1:2, :] = segs_row
    meta[me, 2:3, :] = jnp.broadcast_to(last_seg, (1, tokens))
    for w in loads[6:]:
        w.wait()
    pl.semaphore_wait(barrier, n_seq + n_head - 2)

    def rim_copies(target):
        tail = pl.ds(tokens - RIM, RIM)
        return [
            pltpu.make_async_remote_copy(
                src.at[tail, :], dst, rim_sem.at[0, i], rim_sem.at[1, i], device_id=at_seq(target), device_id_type=MESH
            )
            for i, (src, dst) in enumerate(((inner_ref, rim_inner), (groups_ref, rim_groups)))
        ]

    def meta_copy(slot, other):
        return pltpu.make_async_remote_copy(
            meta.at[slot], meta.at[slot], meta_ss.at[other], meta_rs.at[slot], device_id=at_seq(other), device_id_type=MESH
        )

    def kv_copy(slot, other):
        return pltpu.make_async_remote_copy(
            kv.at[slot, core],
            kv.at[slot, core],
            kv_ss.at[other],
            kv_rs.at[slot],
            device_id=at_seq(other),
            device_id_type=MESH,
        )

    def kv_share(slot):
        return pltpu.make_async_remote_copy(
            kv.at[slot, core],
            kv.at[slot, core],
            share_ss.at[slot],
            share_rs.at[slot],
            device_id=at_head(sibling),
            device_id_type=MESH,
        )

    following = lax.min(me + 1, n_seq - 1)
    previous = lax.max(me - 1, 0)

    @pl.when(me < n_seq - 1)
    def _():
        for c in rim_copies(following):
            c.start()

    def send_meta(d, _):
        meta_copy(me, (me + d) % n_seq).start()
        return 0

    lax.fori_loop(1, n_seq, send_meta, 0)

    def send_kv(k, _):
        kv_copy(me, k).start()
        return 0

    lax.fori_loop(me + 1, n_seq, send_kv, 0)

    pad_inner[RIM:, :] = inner_ref[...].astype(F32)
    pad_groups[RIM:, :] = groups_ref[...].astype(F32)

    @pl.when(me > 0)
    def _():
        meta_copy(previous, previous).wait_recv()
        for c in rim_copies(previous):
            c.wait_recv()

    @pl.when(me == 0)
    def _():
        rim_inner[...] = jnp.zeros_like(rim_inner)
        rim_groups[...] = jnp.zeros_like(rim_groups)

    pad_inner[0:RIM, :] = rim_inner[...].astype(F32)
    pad_groups[0:RIM, :] = rim_groups[...].astype(F32)

    taps = taps_inner_ref.shape[0]
    prev_last = meta[previous, 2:3, 0:1]
    prev_segs = meta[previous, 1:2, :]
    token_col = iota((tokens, 1), 0)
    keeps = []
    for k in range(taps - 1):
        back = taps - 1 - k
        own = jnp.sum(
            jnp.where(row_t - back == col_t, jnp.broadcast_to(segs_row, (tokens, tokens)), 0.0), 1, keepdims=True
        )
        before = jnp.sum(
            jnp.where(row_t - back + tokens == col_t, jnp.broadcast_to(prev_segs, (tokens, tokens)), 0.0),
            1,
            keepdims=True,
        )
        keeps.append(jnp.where(token_col >= back, own, before) == segs_col)

    def conv(pad, weight_ref, out):
        for c in range(0, out.shape[1], LANES):
            cols = slice(c, c + LANES)
            acc = jnp.zeros((tokens, LANES), F32)
            for k in range(taps):
                first = RIM - (taps - 1) + k
                term = weight_ref[k : k + 1, cols] * pad[first : first + tokens, cols]
                acc = acc + (jnp.where(keeps[k], term, 0.0) if k < taps - 1 else term)
            out[:, cols] = jax.nn.silu(acc).astype(BF16)

    conv(pad_groups, taps_groups_ref, conv_bc)
    conv(pad_inner, taps_inner_ref, conv_x)

    read_b = conv_bc[:, :STATE_SIZE]
    read_c = conv_bc[:, STATE_SIZE:]
    in_last = segs_col == last_seg
    tail = jnp.where(in_last, jnp.exp(total_row - cumx[...]), 0.0)
    weighted = (tail * stepx * conv_x[...].astype(F32)).astype(BF16)
    state[...] = dot(read_b, weighted, (0, 0))

    partner = me + 1 - 2 * side
    upper = lax.min(me + 2, n_seq - 1)
    lower = lax.max(me - 2, 0)

    def part(which, c):
        return pl.ds(pl.multiple_of(which * half + c * LANES, LANES), LANES)

    def hop(src, dst, ss, rs, c, target):
        return pltpu.make_async_remote_copy(
            src.at[c], dst.at[c], ss.at[c], rs.at[c], device_id=at_seq(target), device_id_type=MESH
        )

    depth = STATE_SIZE // 2
    for i in range(2 * chunks):
        c, r = i // 2, i % 2
        s_send[i] = state[r * depth : (r + 1) * depth, part(1 - side, c)].astype(BF16)
        hop(s_send, s_recv, s_ss, s_rs, i, partner).start()

    def c_copy():
        return pltpu.make_async_remote_copy(
            conv_bc.at[:, pl.ds(STATE_SIZE, STATE_SIZE)],
            partner_c,
            c_ss.at[0],
            c_rs.at[0],
            device_id=at_seq(partner),
            device_id_type=MESH,
        )

    c_copy().start()

    def wait_meta(d, _):
        k = (me + d) % n_seq
        meta_copy(k, k).wait_recv()
        return 0

    lax.fori_loop(1, n_seq - 1, wait_meta, 0)

    @pl.when(me == 0)
    def _():
        meta_copy(n_seq - 1, n_seq - 1).wait_recv()

    crossing = dot(read_c, read_b, (1, 1))
    live = (jnp.broadcast_to(segs_row, (tokens, tokens)) == segs_col) & (row_t >= col_t)
    left = iota((tokens, LANES), 1) < HEAD_CHANNELS
    for p in range(pairs):
        got = []
        for h in (2 * p, 2 * p + 1):
            decays = jnp.exp(jnp.where(live, cum_cols[:, h : h + 1] - cumul[h : h + 1, :], -jnp.inf))
            mixing = (crossing * decays * steps[h : h + 1, :]).astype(BF16)
            got.append(dot(mixing, conv_x[:, p * LANES : (p + 1) * LANES], (1, 0)))
        y_ref[:, p * LANES : (p + 1) * LANES] = jnp.where(left, got[0], got[1])

    scale = 1.0 / math.sqrt(HD)
    queries = jnp.concatenate([query_ref[:, h * HD : (h + 1) * HD] for h in range(heads_here)], axis=0)
    rows = heads_here * tokens
    segs_rows = jnp.concatenate([segs_col] * heads_here, axis=0)
    token_rows = jnp.concatenate([token_col] * heads_here, axis=0)

    def share(d, _):
        kv_copy(me - d, me).wait_recv()
        kv_share(me - d).start()
        return 0

    def attend(d, carry):
        top, total, summed = carry
        k = me - d

        @pl.when(d > 0)
        def _():
            kv_share(k).wait_recv()

        scores = dot(queries, kv[k, 0], (1, 1)) * scale
        allowed = (meta[k, 1:2, :] == segs_rows) & (
            iota((rows, tokens), 1) + (k - me) * tokens <= token_rows
        )
        scores = jnp.where(allowed, scores, -jnp.inf)
        new_top = jnp.maximum(top, jnp.max(scores, axis=1, keepdims=True))
        rescale = jnp.exp(top - new_top)
        w = jnp.exp(scores - new_top)
        total = total * rescale + jnp.sum(w, axis=1, keepdims=True)
        summed = summed * rescale + dot(w.astype(BF16), kv[k, 1], (1, 0))
        return new_top, total, summed

    def attention():
        lax.fori_loop(1, me + 1, share, 0)
        top, total, summed = lax.fori_loop(
            0,
            me + 1,
            attend,
            (jnp.full((rows, 1), -1e30, F32), jnp.zeros((rows, 1), F32), jnp.zeros((rows, HD), F32)),
        )
        attended = (summed / total).astype(BF16)
        for h in range(heads_here):
            both[:, channels + h * HD : channels + (h + 1) * HD] = attended[h * tokens : (h + 1) * tokens]

    pl.when(me >= n_seq // 2)(attention)

    @pl.when(pair == 0)
    def _():
        e_recv[...] = jnp.zeros_like(e_recv)

    first, second = pair * 2, pair * 2 + 1
    seg_before = meta[lax.max(first - 1, 0), 2:3, 0:1]
    seg_first = meta[first, 2:3, 0:1]
    seg_second = meta[second, 2:3, 0:1]
    through[0:1, :] = jnp.where(
        seg_first == seg_before, jnp.exp(dot(meta[first, 0:1, 0:heads], spread, (1, 0), HIGHEST)), 0.0
    )
    through[1:2, :] = jnp.where(
        seg_second == seg_first, jnp.exp(dot(meta[second, 0:1, 0:heads], spread, (1, 0), HIGHEST)), 0.0
    )
    through[2:3, :] = gain_ref[...].reshape(1, channels)
    c_copy().wait_recv()
    on_left = side == 0
    for c in range(chunks):
        cols = part(side, c)
        through_first = through[0:1, cols]
        through_second = through[1:2, cols]
        theirs = []
        for r in range(2):
            i, span = 2 * c + r, slice(r * depth, (r + 1) * depth)
            hop(s_send, s_recv, s_ss, s_rs, i, partner).wait_recv()
            own, others = state[span, cols], s_recv[i].astype(F32)

            @pl.when(pair > 0)
            def _():
                hop(e_send, e_recv, e_ss, e_rs, i, lower).wait_recv()

            enter_first = e_recv[i].astype(F32)
            enter_second = through_first * enter_first + jnp.where(on_left, own, others)

            @pl.when(pair < last_pair)
            def _():
                e_send[i] = (through_second * enter_second + jnp.where(on_left, others, own)).astype(BF16)
                hop(e_send, e_recv, e_ss, e_rs, i, upper).start()

            theirs.append(jnp.where(on_left, enter_second, enter_first).astype(BF16))
            entering[c, span, :] = jnp.where(on_left, enter_first, enter_second).astype(BF16)

        f_send[c] = dot(partner_c[...], jnp.concatenate(theirs, axis=0), (1, 0)).astype(BF16)
        hop(f_send, f_recv, f_ss, f_rs, c, partner).start()

    joined = segs_col == prev_last
    same_head = (iota((LANES, LANES), 0) // HEAD_CHANNELS == iota((LANES, LANES), 1) // HEAD_CHANNELS).astype(F32)

    def norm(cols, carried):
        y = y_ref[:, cols] + jnp.where(joined, jnp.exp(cumx[:, cols]), 0.0) * carried
        gated = y * jax.nn.silu(gate_ref[:, cols].astype(F32))
        mean_square = dot(gated * gated, same_head, (1, 0), HIGHEST) * (1.0 / HEAD_CHANNELS)
        both[:, cols] = (gated * lax.rsqrt(mean_square + 1e-05) * through[2:3, cols]).astype(BF16)

    pl.when(me < n_seq // 2)(attention)
    for c in range(chunks):
        norm(part(side, c), dot(read_c, entering[c], (1, 0)))
    for c in range(chunks):
        hop(f_send, f_recv, f_ss, f_rs, c, partner).wait_recv()
        norm(part(1 - side, c), f_recv[c].astype(F32))

    for w in weights:
        w.wait()
    width = out_ref.shape[1]

    def product(j, part_of):
        cols = pl.ds(pl.multiple_of(j * width + part_of * (width // 2), LANES), width // 2)
        return dot(both[:, :channels], mproj[:, cols], (1, 0)) + dot(both[:, channels:], aproj[:, cols], (1, 0))

    def rs_copy(i, target):
        return pltpu.make_async_remote_copy(
            rs_send.at[i], rs_recv.at[i], rs_ss.at[i], rs_rs.at[i], device_id=at_head(target), device_id_type=MESH
        )

    to_pair = [rs_copy(h, sibling) for h in range(2)]
    to_sibling = [rs_copy(2 + h, sibling) for h in range(2)]
    to_opposite = [rs_copy(4 + h, opposite) for h in range(2)]
    for h in range(2):
        rs_send[h] = product(opposite_sibling, h).astype(BF16)
        to_pair[h].start()
    for h in range(2):
        away = product(opposite, h)
        to_pair[h].wait_recv()
        rs_send[4 + h] = (away + rs_recv[h].astype(F32)).astype(BF16)
        to_opposite[h].start()
    for h in range(2):
        rs_send[2 + h] = product(sibling, h).astype(BF16)
        to_sibling[h].start()
    for h in range(2):
        result = product(mine, h)
        to_sibling[h].wait_recv()
        result = result + rs_recv[2 + h].astype(F32)
        to_opposite[h].wait_recv()
        out_ref[:, h * (width // 2) : (h + 1) * (width // 2)] = (result + rs_recv[4 + h].astype(F32)).astype(BF16)

    for copy in (*to_pair, *to_sibling, *to_opposite, c_copy()):
        copy.wait_send()

    def sent_share(d, _):
        kv_share(me - d).wait_send()
        return 0

    lax.fori_loop(1, me + 1, sent_share, 0)

    @pl.when(me < n_seq - 1)
    def _():
        for c in rim_copies(following):
            c.wait_send()

    def sent_meta(d, _):
        meta_copy(me, (me + d) % n_seq).wait_send()
        return 0

    lax.fori_loop(1, n_seq, sent_meta, 0)

    def sent_kv(k, _):
        kv_copy(me, k).wait_send()
        return 0

    lax.fori_loop(me + 1, n_seq, sent_kv, 0)
    for c in range(chunks):
        hop(f_send, f_recv, f_ss, f_rs, c, partner).wait_send()
    for i in range(2 * chunks):
        hop(s_send, s_recv, s_ss, s_rs, i, partner).wait_send()

        @pl.when(pair < last_pair)
        def _():
            hop(e_send, e_recv, e_ss, e_rs, i, upper).wait_send()


def shards(n_seq, n_head, *arrays):
    (inner, groups, gate, step, bias, decay, taps_i, taps_g, gain, query, key, value, segs, mproj, aproj) = arrays
    tokens, channels = inner.shape
    out_width = mproj.shape[1] // n_head
    chunks = channels // 2 // LANES
    hops = (chunks, STATE_SIZE, LANES)
    vmem = pl.BlockSpec(memory_space=pltpu.VMEM)
    hbm = pl.BlockSpec(memory_space=pltpu.HBM)
    dma = pltpu.SemaphoreType.DMA
    scratch = [
        *[pltpu.VMEM(a.shape, a.dtype) for a in arrays[:13]],
        pltpu.VMEM(mproj.shape, BF16),
        pltpu.VMEM(aproj.shape, BF16),
        pltpu.VMEM((tokens + RIM, channels), F32),
        pltpu.VMEM((tokens + RIM, groups.shape[1]), F32),
        pltpu.VMEM((RIM, channels), BF16),
        pltpu.VMEM((RIM, groups.shape[1]), BF16),
        pltpu.VMEM((n_seq, 8, tokens), F32),
        pltpu.VMEM((n_seq, 2, tokens, HD), BF16),
        pltpu.VMEM((tokens, channels), BF16),
        pltpu.VMEM((tokens, groups.shape[1]), BF16),
        pltpu.VMEM((tokens, channels), F32),
        pltpu.VMEM((tokens, channels), F32),
        pltpu.VMEM((STATE_SIZE, channels), F32),
        *[pltpu.VMEM((2 * chunks, STATE_SIZE // 2, LANES), BF16) for _ in range(4)],
        *[pltpu.VMEM((chunks, tokens, LANES), BF16) for _ in range(2)],
        pltpu.VMEM((tokens, STATE_SIZE), BF16),
        pltpu.VMEM(hops, BF16),
        pltpu.VMEM((8, channels), F32),
        pltpu.VMEM((tokens, channels + query.shape[1]), BF16),
        pltpu.VMEM((6, tokens, out_width // 2), BF16),
        pltpu.VMEM((6, tokens, out_width // 2), BF16),
        dma((13,)),
        dma((2,)),
        dma((2, 2)),
        dma((n_seq,)),
        dma((n_seq,)),
        dma((n_seq,)),
        dma((n_seq,)),
        dma((n_seq,)),
        dma((n_seq,)),
        dma((1,)),
        dma((1,)),
        *[dma((2 * chunks,)) for _ in range(4)],
        *[dma((chunks,)) for _ in range(2)],
        dma((6,)),
        dma((6,)),
    ]
    return pl.pallas_call(
        functools.partial(kernel, n_seq, n_head),
        out_shape=jax.ShapeDtypeStruct((tokens, out_width), BF16),
        in_specs=[hbm] * 15,
        out_specs=vmem,
        scratch_shapes=scratch,
        compiler_params=pltpu.CompilerParams(
            collective_id=0, has_side_effects=True, vmem_limit_bytes=64 * 2**20
        ),
        name="mixer",
    )(
        inner,
        groups,
        gate,
        step,
        bias,
        decay,
        taps_i,
        taps_g,
        gain,
        query,
        key,
        value,
        segs,
        mproj,
        aproj,
    )


def solution(mesh):
    placed = (
        P("seq", "head"),
        P("seq", None),
        P("seq", "head"),
        P("head", "seq"),
        P("head"),
        P("head"),
        P(None, "head"),
        P(),
        P("head"),
        P("seq", "head"),
        P("seq", None),
        P("seq", None),
        P("seq"),
        P("head", None),
        P("head", None),
    )
    return jax.shard_map(
        functools.partial(shards, mesh.shape["seq"], mesh.shape["head"]),
        mesh=mesh,
        in_specs=placed,
        out_specs=P("seq", "head"),
        check_vma=False,
    )
```
